512 devices in a mesh: lat: 32 (over z_lo, x, core), chan: 16 (over z_hi, y).
Axes of the slice: x: 4, y: 8, z: 8 (z_hi: 2, z_lo: 4; z = z_hi * 4 + z_lo), core: 2. Of those that a mesh axis runs over, the one named last changes fastest.
Arguments:
- atmosphere: bfloat16 [256, 256, 1536], P('chan', 'lat'), may hold values from -6 to 6
- first_weight: bfloat16 [256, 16, 5, 5], P('chan'), may hold values from -0.3125 to 0.3125
- first_bias: float32 [256], P('chan'), may hold values from -3 to 3
- second_weight: bfloat16 [256, 16, 5, 5], P('chan'), may hold values from -0.3125 to 0.3125
Outputs:
- spectrum: float32 [128, 2, 256, 2, 128], P('lat', None, 'chan')
The draws below stay inside these ranges and needn't reach their ends.
All inputs are finite; a program needn't handle non-finite values.
Results may differ from the reference program's by a relative error of at most 0.007.
Values may be sent and summed in bfloat16 or wider, within the bound.
A program may use at most 64 MiB of HBM per device.

```python
import math
import jax
import jax.numpy as jnp
from jax import lax

CHANNELS = 256
GROUP = 16
KERNEL = 5
LON = 1536
ORDERS = 128
DEGREES = 256
LAT = 256


def block_scale(rng, extent, split, least, high):
    gain = 1.0
    for axis_at, blocks in split:
        steps = jax.random.uniform(jax.random.fold_in(jax.random.fold_in(rng, 6), axis_at), (blocks,), jnp.float32, least / len(split), high / len(split))
        gain = gain * jnp.repeat(jnp.exp(steps), extent[axis_at] // blocks).reshape((-1,) + (1,) * (len(extent) - 1 - axis_at))
    return gain


def centred(key, extent, scale, most, split=(), held_as=jnp.bfloat16):
    drawn = scale * jax.random.normal(key, extent, jnp.float32)
    if split:
        drawn = drawn * block_scale(key, extent, split, -0.22, 0.18)
    return jnp.clip(drawn, -most, most).astype(held_as)


def setup_inputs(seed: int = 0) -> dict:
    seeds = jax.random.split(jax.random.key(seed), 5)
    atmosphere = centred(seeds[0], (CHANNELS, LAT, LON), 1.0, 6.0, ((0, 16), (1, 32)))
    first_weight = centred(seeds[1], (CHANNELS, GROUP, KERNEL, KERNEL), (GROUP * KERNEL * KERNEL) ** -0.5, 0.3125, ((0, 16),))
    first_bias = centred(seeds[2], (CHANNELS,), 0.5, 3.0, ((0, 16),), jnp.float32)
    second_weight = centred(seeds[3], (CHANNELS, GROUP, KERNEL, KERNEL), (GROUP * KERNEL * KERNEL) ** -0.5, 0.3125, ((0, 16),))
    return {"atmosphere": atmosphere, "first_weight": first_weight, "first_bias": first_bias, "second_weight": second_weight}


def fourier_table(length, orders):
    places = lax.broadcasted_iota(jnp.int32, (length, orders), 0)
    numbers = lax.broadcasted_iota(jnp.int32, (length, orders), 1) + 1
    phases = (places * numbers % length).astype(jnp.float32) * (2.0 * math.pi / length)
    factor = 1.0 / math.sqrt(length)
    return (jnp.concatenate([jnp.cos(phases), -jnp.sin(phases)], axis=1) * factor).astype(jnp.bfloat16)

def legendre(colatitude, orders, degrees):
    cosine = jnp.cos(colatitude)[None, :]
    sines = jnp.sin(colatitude)[None, :]
    order_real = orders.astype(jnp.float32)[:, None]
    log_diag = 0.5 * (jnp.log((2.0 * order_real + 1.0) / 2.0) + lax.lgamma(2.0 * order_real + 1.0) - order_real * math.log(4.0) - 2.0 * lax.lgamma(order_real + 1.0)) + order_real * jnp.log(sines)
    diagonal = jnp.exp(log_diag)
    empty_rows = jnp.zeros_like(diagonal)

    def advance(carried, degree):
        latest, before = carried
        degree_real = degree.astype(jnp.float32)
        spread = jnp.maximum(degree_real * degree_real - order_real * order_real, 1.0)
        raising = jnp.sqrt(jnp.maximum(4.0 * degree_real * degree_real - 1.0, 1.0) / spread)
        previous = degree_real - 1.0
        lowering = jnp.sqrt(jnp.maximum(previous * previous - order_real * order_real, 0.0) / jnp.maximum(4.0 * previous * previous - 1.0, 1.0))
        raised = raising * (cosine * latest - lowering * before)
        result = jnp.where(degree_real == order_real, diagonal, jnp.where(degree_real > order_real, raised, 0.0))
        return ((result, latest), result)
    _, stacked = lax.scan(advance, (empty_rows, empty_rows), jnp.arange(degrees, dtype=jnp.int32), unroll=16)
    return stacked

def weighted_table(north_rows, orders, total_rows, degrees):
    colatitude = math.pi * (north_rows.astype(jnp.float32) + 0.5) / total_rows
    quadrature = math.pi * jnp.sin(colatitude) / math.sqrt(total_rows)
    return legendre(colatitude, orders, degrees) * quadrature[None, None, :]

def project_exact(even_sum, odd_sum, stacked, orders):
    degrees, number, height = stacked.shape
    paired = stacked.reshape(degrees // 2, 2, number, height).transpose(2, 1, 3, 0).astype(jnp.bfloat16)
    parity = (orders[:, None] + jnp.arange(2, dtype=jnp.int32)[None, :]) % 2 == 0
    selected = jnp.where(parity, even_sum[..., None], odd_sum[..., None])
    return jnp.einsum('crakq,kqrj->kqcaj', selected.astype(jnp.float32), paired.astype(jnp.float32), precision=lax.Precision.HIGHEST)

def convolve(padded, kernel):
    radius = kernel.shape[3] // 2
    widened = jnp.concatenate([padded[..., -radius:], padded, padded[..., :radius]], axis=2)
    result = lax.conv_general_dilated(widened[None], kernel, (1, 1), 'VALID', feature_group_count=padded.shape[0] // kernel.shape[1], precision=lax.Precision.HIGHEST)
    return result[0]

def reference(atmosphere, first_weight, first_bias, second_weight):
    halfway = LAT // 2
    radius = KERNEL // 2
    groups = CHANNELS // GROUP
    fourier = fourier_table(LON, ORDERS)
    orders = jnp.arange(1, ORDERS + 1, dtype=jnp.int32)
    spherical = weighted_table(jnp.arange(halfway, dtype=jnp.int32), orders, LAT, DEGREES)

    def per_group(pieces):
        group_block, kernel_one, offsets, kernel_two = pieces
        inputs = group_block.astype(jnp.float32)
        padded = jnp.pad(inputs, ((0, 0), (radius, radius), (0, 0)))
        hidden = jax.nn.gelu(convolve(padded, kernel_one.astype(jnp.float32)) + offsets[:, None, None], approximate=False).astype(jnp.bfloat16)
        padded = jnp.pad(hidden.astype(jnp.float32), ((0, 0), (radius, radius), (0, 0)))
        updated = (inputs + convolve(padded, kernel_two.astype(jnp.float32))).astype(jnp.bfloat16)
        spectra = jnp.dot(updated.reshape(GROUP * LAT, LON), fourier, preferred_element_type=jnp.float32)
        spectra = spectra.astype(jnp.bfloat16).reshape(GROUP, LAT, 2, ORDERS)
        northern = spectra[:, :halfway].astype(jnp.float32)
        southern = spectra[:, halfway:][:, ::-1].astype(jnp.float32)
        even_sum = (northern + southern).astype(jnp.bfloat16)
        odd_sum = (northern - southern).astype(jnp.bfloat16)
        return project_exact(even_sum, odd_sum, spherical, orders)
    stacked = lax.map(per_group, (atmosphere.reshape(groups, GROUP, LAT, LON), first_weight.reshape(groups, GROUP, GROUP, KERNEL, KERNEL), first_bias.reshape(groups, GROUP), second_weight.reshape(groups, GROUP, GROUP, KERNEL, KERNEL)))
    return stacked.transpose(1, 2, 0, 3, 4, 5).reshape(ORDERS, 2, CHANNELS, 2, DEGREES // 2)
```

```python
import functools
import math

import jax
import jax.numpy as jnp
import numpy as np
from jax import lax
from jax.experimental import pallas as pl
from jax.experimental.pallas import tpu as pltpu
from jax.sharding import PartitionSpec as P

ORDERS = 128
DEGREES = 256
LAT = 256
LON = 1536
BANDS = 32
ROWS = 8
CH = 16
OWN = ORDERS // BANDS
BF16 = jnp.bfloat16
F32 = jnp.float32


def fourier_rows():
    orders = np.arange(1, ORDERS + 1)
    places = np.arange(LON)
    phases = (orders[:, None] * places[None, :] % LON) * (2.0 * math.pi / LON)
    real = np.cos(phases) / math.sqrt(LON)
    imag = -np.sin(phases) / math.sqrt(LON)
    both = np.stack([real.reshape(BANDS, OWN, LON), imag.reshape(BANDS, OWN, LON)], axis=1)
    return both.reshape(2 * ORDERS, LON).astype(BF16)


def phase_rows():
    orders = np.arange(1, ORDERS + 1).reshape(BANDS, OWN)
    out = []
    for step in (1, 2):
        angle = 2.0 * math.pi * step * orders / LON
        cosine = np.stack([np.cos(angle), np.cos(angle)], axis=1).reshape(2 * ORDERS)
        sine = np.stack([-np.sin(angle), np.sin(angle)], axis=1).reshape(2 * ORDERS)
        out += [cosine, sine]
    table = np.stack(out)[:, :, None]
    return np.broadcast_to(table, (4, 2 * ORDERS, 128)).astype(np.float32).copy()


def projection_table():
    half = LAT // 2
    single = np.float32
    theta = (math.pi * (np.arange(half) + 0.5) / LAT).astype(single)
    cosine, sine = np.cos(theta)[None, :], np.sin(theta)[None, :]
    order = np.arange(1, ORDERS + 1, dtype=single)[:, None]
    gamma = np.vectorize(math.lgamma, otypes=[single])
    log_diag = (
        single(0.5)
        * (
            np.log((2 * order + 1) / 2)
            + gamma(2 * order + 1)
            - order * single(math.log(4.0))
            - 2 * gamma(order + 1)
        )
        + order * np.log(sine)
    )

    def normal(value):
        return np.where(np.abs(value) < np.finfo(single).tiny, single(0.0), value)

    diagonal = normal(np.exp(log_diag))
    latest = np.zeros_like(diagonal)
    before = np.zeros_like(diagonal)
    stacked = np.zeros((DEGREES, ORDERS, half), single)
    for degree in range(DEGREES):
        real = single(degree)
        spread = np.maximum(real * real - order * order, single(1.0))
        raising = np.sqrt(np.maximum(4 * real * real - 1, single(1.0)) / spread)
        previous = real - 1
        lowering = np.sqrt(
            np.maximum(previous * previous - order * order, single(0.0))
            / np.maximum(4 * previous * previous - 1, single(1.0))
        )
        raised = normal(
            raising * normal(normal(cosine * latest) - normal(lowering * before))
        )
        result = np.where(order == real, diagonal, np.where(order < real, raised, single(0.0)))
        stacked[degree] = result
        latest, before = result, latest
    weighted = stacked * (single(math.pi) * sine / single(math.sqrt(LAT)))[None]
    weighted = weighted.astype(BF16).astype(single)
    degrees = np.arange(DEGREES)[:, None, None]
    numbers = np.arange(1, ORDERS + 1)[None, :, None]
    sign = np.where((degrees + numbers) % 2 == 0, 1.0, -1.0).astype(np.float32)
    whole = np.concatenate([weighted, (weighted * sign)[:, :, ::-1]], axis=2)
    whole = whole.reshape(DEGREES // 2, 2, ORDERS, LAT).transpose(2, 3, 1, 0)
    return whole.reshape(BANDS, OWN, LAT, DEGREES).astype(BF16)


EDGE = (0, 1, 6, 7)
SLOTS = (0, 1, 2, 3, 4, 5, 6, 7, 8, 9, -2, -1)


def spread_first():
    own = np.zeros((128, ROWS, CH, ROWS), np.float32)
    halo = np.zeros((128, 4, 2, CH, 2), np.float32)
    for dy in range(5):
        for i in range(CH):
            for y in range(ROWS):
                row = y + dy - 2
                if 0 <= row < ROWS:
                    own[dy * CH + i, y, i, row] = 1.0
                elif row < 0:
                    halo[dy * CH + i, EDGE.index(y), 0, i, row + 2] = 1.0
                else:
                    halo[dy * CH + i, EDGE.index(y), 1, i, row - ROWS] = 1.0
    return np.concatenate([own.reshape(128, -1), halo.reshape(128, -1)], axis=1).astype(BF16)


def spread_second():
    out = np.zeros((128, len(SLOTS), ROWS, CH), np.float32)
    for dy in range(5):
        for i in range(CH):
            for at, slot in enumerate(SLOTS):
                row = slot + dy - 2
                if 0 <= row < ROWS:
                    out[dy * CH + i, at, row, i] = 1.0
    return out.reshape(128, -1).astype(BF16)


def edge_rows():
    out = np.zeros((2, CH, 2, CH, ROWS), np.float32)
    for c in range(CH):
        for t in range(2):
            out[0, c, t, c, t] = 1.0
            out[1, c, t, c, ROWS - 2 + t] = 1.0
    return out.reshape(64, 128).astype(BF16)


def placed_rows():
    out = np.zeros((16, CH, CH, ROWS), np.float32)
    for c in range(CH):
        for y in range(ROWS):
            out[y, c, c, y] = 1.0
    return out.reshape(256, 128).astype(BF16)


def nt(a, b):
    return lax.dot_general(a, b, (((1,), (1,)), ((), ())), preferred_element_type=F32)


def gelu(x):
    return 0.5 * x * (1.0 + lax.erf(x * math.sqrt(0.5)))


def swap_blocks(x):
    sub = lax.broadcasted_iota(jnp.int32, x.shape, 1)
    block = lax.broadcasted_iota(jnp.int32, x.shape, 2) // CH
    for bit in (1, 2, 4):
        high_sub = (sub & bit) != 0
        high_block = (block & bit) != 0
        lane = CH * bit
        down = pltpu.roll(pltpu.roll(x, 8 - bit, 1), lane, 2)
        up = pltpu.roll(pltpu.roll(x, bit, 1), 128 - lane, 2)
        x = jnp.where(high_sub == high_block, x, jnp.where(high_sub, up, down))
    return x


def base_of(weight):
    pieces = [weight[dy].reshape(5 * CH, CH).astype(F32) for dy in range(5)]
    pieces.append(jnp.zeros((5 * CH, 128 - 5 * CH), F32))
    return jnp.concatenate(pieces, axis=1).astype(BF16)


def kernel(
    atm, w1, bias, w2, edge, spread1, spread2, placed, fourier, phase, table, out,
    shifted, halo, w1_v, bias_v, w2_v, edge_v, spread1_v, spread2_v, fourier_v, phase_v, table_v,
    t1, t1h, t2, hsend, acc, hidden, mixed, packed, received, result,
    load_sem, halo_send, halo_recv, a2a_send, a2a_recv, out_sem,
):
    me = lax.axis_index("lat")
    barrier = pltpu.get_barrier_semaphore()

    loads = [
        (atm, shifted.at[pl.ds(256, 128), :]),
        (edge, edge_v),
        (w1, w1_v),
        (spread1, spread1_v),
        (bias, bias_v),
        (w2, w2_v),
        (spread2, spread2_v),
        (fourier, fourier_v),
        (placed, t2.at[:, pl.ds(640, 128)]),
        (phase, phase_v),
        (table.at[me], table_v),
    ]
    copies = [
        pltpu.make_async_copy(source, target, load_sem.at[n])
        for n, (source, target) in enumerate(loads)
    ]
    for copy in copies:
        copy.start()

    def greet(j, carry):
        pl.semaphore_signal(
            barrier, inc=1, device_id={"lat": lax.rem(me + j, BANDS)},
            device_id_type=pl.DeviceIdType.MESH,
        )
        return carry

    lax.fori_loop(1, BANDS, greet, 0)

    copies[0].wait()
    copies[1].wait()
    hsend[...] = jnp.dot(
        edge_v[...], shifted[256:384, :], preferred_element_type=F32
    ).astype(BF16)

    pl.semaphore_wait(barrier, BANDS - 1)

    up = lax.max(me - 1, 0)
    down = lax.min(me + 1, BANDS - 1)
    to_up = pltpu.make_async_remote_copy(
        src_ref=hsend.at[pl.ds(0, 32), :], dst_ref=halo.at[pl.ds(160, 32), :],
        send_sem=halo_send.at[0], recv_sem=halo_recv.at[0],
        device_id={"lat": up}, device_id_type=pl.DeviceIdType.MESH,
    )
    to_down = pltpu.make_async_remote_copy(
        src_ref=hsend.at[pl.ds(32, 32), :], dst_ref=halo.at[pl.ds(128, 32), :],
        send_sem=halo_send.at[1], recv_sem=halo_recv.at[1],
        device_id={"lat": down}, device_id_type=pl.DeviceIdType.MESH,
    )

    @pl.when(me > 0)
    def _():
        to_up.start()

    @pl.when(me < BANDS - 1)
    def _():
        to_down.start()

    copies[2].wait()
    copies[3].wait()
    res1 = jnp.dot(base_of(w1_v), spread1_v[...], preferred_element_type=F32).astype(BF16)
    for dx in range(5):
        for y in range(ROWS):
            t1[16 * y : 16 * y + 16, 128 * dx : 128 * dx + 128] = res1[
                16 * dx : 16 * dx + 16, 128 * y : 128 * y + 128
            ]
        for e in range(4):
            t1h[16 * e : 16 * e + 16, 64 * dx : 64 * dx + 64] = res1[
                16 * dx : 16 * dx + 16, 1024 + 64 * e : 1088 + 64 * e
            ]

    own = shifted[256:384, :].astype(F32)
    for dx in (0, 1, 3, 4):
        shifted[128 * dx : 128 * dx + 128, :] = pltpu.roll(own, (2 - dx) % LON, 1).astype(BF16)
    copies[4].wait()
    eye = lax.broadcasted_iota(jnp.int32, (CH, CH), 0) == lax.broadcasted_iota(
        jnp.int32, (CH, CH), 1
    )
    column = jnp.sum(
        jnp.where(eye, jnp.broadcast_to(bias_v[...], (CH, CH)), 0.0), axis=1, keepdims=True
    )
    offsets = jnp.concatenate([column] * ROWS, axis=0)
    acc[...] = jnp.dot(t1[...], shifted[...], preferred_element_type=F32) + offsets
    hidden[32:96, :] = gelu(acc[32:96, :]).astype(BF16)

    copies[5].wait()
    copies[6].wait()
    res2 = jnp.dot(base_of(w2_v), spread2_v[...], preferred_element_type=F32).astype(BF16)
    for at, slot in enumerate(SLOTS):
        row = 16 * (slot % 16)
        for dx in range(5):
            t2[row : row + 16, 128 * dx : 128 * dx + 128] = res2[
                16 * dx : 16 * dx + 16, 128 * at : 128 * at + 128
            ]
    t2[160:224, 0:640] = jnp.zeros((64, 640), BF16)
    copies[7].wait()
    mixed[:, 640:768] = nt(fourier_v[...], shifted[256:384, :]).astype(BF16)

    @pl.when(me > 0)
    def _():
        to_up.wait_send()
        to_down.wait_recv()

    @pl.when(me < BANDS - 1)
    def _():
        to_down.wait_send()
        to_up.wait_recv()

    @pl.when(me == 0)
    def _():
        halo[128:160, :] = jnp.zeros((32, LON), BF16)

    @pl.when(me == BANDS - 1)
    def _():
        halo[160:192, :] = jnp.zeros((32, LON), BF16)

    rim = halo[128:192, :].astype(F32)
    for dx in (0, 1, 3, 4):
        halo[64 * dx : 64 * dx + 64, :] = pltpu.roll(rim, (2 - dx) % LON, 1).astype(BF16)
    more = jnp.dot(t1h[...], halo[...], preferred_element_type=F32)
    hidden[0:32, :] = gelu(acc[0:32, :] + more[0:32]).astype(BF16)
    hidden[96:128, :] = gelu(acc[96:128, :] + more[32:64]).astype(BF16)

    spectra = nt(fourier_v[...], hidden[...])
    swapped = pltpu.roll(spectra.reshape(BANDS, 8, 128), 4, 1).reshape(256, 128)
    copies[9].wait()
    mixed[:, 256:384] = spectra.astype(BF16)
    for step, low, high in ((1, 1, 3), (2, 0, 4)):
        straight = phase_v[2 * step - 2] * spectra
        crossed = phase_v[2 * step - 1] * swapped
        mixed[:, 128 * high : 128 * high + 128] = (straight + crossed).astype(BF16)
        mixed[:, 128 * low : 128 * low + 128] = (straight - crossed).astype(BF16)

    copies[8].wait()
    sums = nt(mixed[...], t2[...]).reshape(BANDS, 8, 256)
    near = swap_blocks(sums[:, :, 0:128])
    far = swap_blocks(sums[:, :, 128:256])
    packed[...] = jnp.concatenate([near, far], axis=1).astype(BF16)

    def send(j, carry):
        p = lax.rem(me + j, BANDS)
        pltpu.make_async_remote_copy(
            src_ref=packed.at[p], dst_ref=received.at[me],
            send_sem=a2a_send, recv_sem=a2a_recv,
            device_id={"lat": p}, device_id_type=pl.DeviceIdType.MESH,
        ).start()
        return carry

    lax.fori_loop(1, BANDS, send, 0)
    received[me] = packed[me]
    copies[10].wait()
    some = pltpu.make_async_remote_copy(
        src_ref=packed.at[pl.ds(0, BANDS - 1)], dst_ref=received.at[pl.ds(0, BANDS - 1)],
        send_sem=a2a_send, recv_sem=a2a_recv,
        device_id={"lat": lax.rem(me + 1, BANDS)}, device_id_type=pl.DeviceIdType.MESH,
    )
    some.wait_recv()

    parts = received[...].astype(F32)
    near = parts[:, 0:8, :]
    far = parts[:, 8:16, :]
    none = jnp.zeros((1, 8, 128), F32)
    above = jnp.concatenate([none, far[:-1]], axis=0)
    below = jnp.concatenate([far[1:], none], axis=0)
    first = lax.broadcasted_iota(jnp.int32, near.shape, 1) < 4
    rows = (near + jnp.where(first, above, below)).reshape(LAT, 128)
    lines = rows.T.astype(BF16)
    for m in range(OWN):
        left = jnp.concatenate([lines[16 * m : 16 * m + 16], lines[64 + 16 * m : 80 + 16 * m]], axis=0)
        done = jnp.dot(left, table_v[m], preferred_element_type=F32)
        for q in range(2):
            for a in range(2):
                result[m, q, pl.ds(a, CH, stride=2), :] = done[
                    16 * a : 16 * a + 16, 128 * q : 128 * q + 128
                ]
    finish = pltpu.make_async_copy(result, out, out_sem)
    finish.start()
    finish.wait()
    some.wait_send()


@functools.cache
def constants():
    return (
        edge_rows(), spread_first(), spread_second(), placed_rows(), fourier_rows(),
        phase_rows(), projection_table(),
    )


def per_device(atmosphere, first_weight, first_bias, second_weight):
    edge, spread1, spread2, placed, fourier, phase, table = constants()
    operands = (
        atmosphere.reshape(CH * ROWS, LON),
        first_weight.transpose(2, 3, 0, 1),
        first_bias.reshape(1, CH),
        second_weight.transpose(2, 3, 0, 1),
        edge, spread1, spread2, placed, fourier, phase, table,
    )
    scratch = [
        pltpu.VMEM((640, LON), BF16),
        pltpu.VMEM((320, LON), BF16),
        pltpu.VMEM((5, 5, CH, CH), BF16),
        pltpu.VMEM((1, CH), F32),
        pltpu.VMEM((5, 5, CH, CH), BF16),
        pltpu.VMEM(edge.shape, BF16),
        pltpu.VMEM(spread1.shape, BF16),
        pltpu.VMEM(spread2.shape, BF16),
        pltpu.VMEM(fourier.shape, BF16),
        pltpu.VMEM(phase.shape, F32),
        pltpu.VMEM(table.shape[1:], BF16),
        pltpu.VMEM((128, 640), BF16),
        pltpu.VMEM((64, 320), BF16),
        pltpu.VMEM((256, 768), BF16),
        pltpu.VMEM((64, LON), BF16),
        pltpu.VMEM((128, LON), F32),
        pltpu.VMEM((128, LON), BF16),
        pltpu.VMEM((256, 768), BF16),
        pltpu.VMEM((BANDS, 16, 128), BF16),
        pltpu.VMEM((BANDS, 16, 128), BF16),
        pltpu.VMEM((OWN, 2, 2 * CH, 128), F32),
        pltpu.SemaphoreType.DMA((11,)),
        pltpu.SemaphoreType.DMA((2,)),
        pltpu.SemaphoreType.DMA((2,)),
        pltpu.SemaphoreType.DMA,
        pltpu.SemaphoreType.DMA,
        pltpu.SemaphoreType.DMA,
    ]
    spectrum = pl.pallas_call(
        kernel,
        out_shape=jax.ShapeDtypeStruct((OWN, 2, 2 * CH, 128), F32),
        in_specs=[pl.BlockSpec(memory_space=pl.ANY)] * len(operands),
        out_specs=pl.BlockSpec(memory_space=pl.ANY),
        scratch_shapes=scratch,
        compiler_params=pltpu.CompilerParams(
            collective_id=0, has_side_effects=True, vmem_limit_bytes=56 * 1024 * 1024
        ),
        name="encoder",
    )(*operands)
    return spectrum.reshape(OWN, 2, CH, 2, 128)


def solution(mesh):
    placed = (
        P("chan", "lat", None),
        P("chan", None, None, None),
        P("chan"),
        P("chan", None, None, None),
    )
    return jax.shard_map(
        per_device,
        mesh=mesh,
        in_specs=placed,
        out_specs=P("lat", None, "chan", None, None),
        check_vma=False,
    )
```

```python
import functools
import math

import jax
import jax.numpy as jnp
import numpy as np
from jax import lax
from jax.experimental import pallas as pl
from jax.experimental.pallas import tpu as pltpu
from jax.sharding import PartitionSpec as P

ORDERS = 128
DEGREES = 256
LAT = 256
LON = 1536
BANDS = 32
ROWS = 8
CH = 16
OWN = ORDERS // BANDS
BF16 = jnp.bfloat16
F32 = jnp.float32


def fourier_rows():
    orders = np.arange(1, ORDERS + 1)
    places = np.arange(LON)
    phases = (orders[:, None] * places[None, :] % LON) * (2.0 * math.pi / LON)
    real = np.cos(phases) / math.sqrt(LON)
    imag = -np.sin(phases) / math.sqrt(LON)
    both = np.stack([real.reshape(BANDS, OWN, LON), imag.reshape(BANDS, OWN, LON)], axis=1)
    return both.reshape(2 * ORDERS, LON).astype(BF16)


def phase_rows():
    orders = np.arange(1, ORDERS + 1).reshape(BANDS, OWN)
    out = []
    for step in (1, 2):
        angle = 2.0 * math.pi * step * orders / LON
        cosine = np.stack([np.cos(angle), np.cos(angle)], axis=1).reshape(2 * ORDERS)
        sine = np.stack([-np.sin(angle), np.sin(angle)], axis=1).reshape(2 * ORDERS)
        out += [cosine, sine]
    table = np.stack(out)[:, :, None]
    return np.broadcast_to(table, (4, 2 * ORDERS, 128)).astype(np.float32).copy()


def projection_table():
    half = LAT // 2
    single = np.float32
    theta = (math.pi * (np.arange(half) + 0.5) / LAT).astype(single)
    cosine, sine = np.cos(theta)[None, :], np.sin(theta)[None, :]
    order = np.arange(1, ORDERS + 1, dtype=single)[:, None]
    gamma = np.vectorize(math.lgamma, otypes=[single])
    log_diag = (
        single(0.5)
        * (
            np.log((2 * order + 1) / 2)
            + gamma(2 * order + 1)
            - order * single(math.log(4.0))
            - 2 * gamma(order + 1)
        )
        + order * np.log(sine)
    )

    def normal(value):
        return np.where(np.abs(value) < np.finfo(single).tiny, single(0.0), value)

    diagonal = normal(np.exp(log_diag))
    latest = np.zeros_like(diagonal)
    before = np.zeros_like(diagonal)
    stacked = np.zeros((DEGREES, ORDERS, half), single)
    for degree in range(DEGREES):
        real = single(degree)
        spread = np.maximum(real * real - order * order, single(1.0))
        raising = np.sqrt(np.maximum(4 * real * real - 1, single(1.0)) / spread)
        previous = real - 1
        lowering = np.sqrt(
            np.maximum(previous * previous - order * order, single(0.0))
            / np.maximum(4 * previous * previous - 1, single(1.0))
        )
        raised = normal(
            raising * normal(normal(cosine * latest) - normal(lowering * before))
        )
        result = np.where(order == real, diagonal, np.where(order < real, raised, single(0.0)))
        stacked[degree] = result
        latest, before = result, latest
    weighted = stacked * (single(math.pi) * sine / single(math.sqrt(LAT)))[None]
    weighted = weighted.astype(BF16).astype(single)
    degrees = np.arange(DEGREES)[:, None, None]
    numbers = np.arange(1, ORDERS + 1)[None, :, None]
    sign = np.where((degrees + numbers) % 2 == 0, 1.0, -1.0).astype(np.float32)
    whole = np.concatenate([weighted, (weighted * sign)[:, :, ::-1]], axis=2)
    whole = whole.reshape(DEGREES // 2, 2, ORDERS, LAT).transpose(2, 3, 1, 0)
    return whole.reshape(BANDS, OWN, LAT, DEGREES).astype(BF16)


EDGE = (0, 1, 6, 7)
SLOTS = (0, 1, 2, 3, 4, 5, 6, 7, 8, 9, -2, -1)


def spread_first():
    own = np.zeros((128, ROWS, CH, ROWS), np.float32)
    halo = np.zeros((128, 4, 2, CH, 2), np.float32)
    for dy in range(5):
        for i in range(CH):
            for y in range(ROWS):
                row = y + dy - 2
                if 0 <= row < ROWS:
                    own[dy * CH + i, y, i, row] = 1.0
                elif row < 0:
                    halo[dy * CH + i, EDGE.index(y), 0, i, row + 2] = 1.0
                else:
                    halo[dy * CH + i, EDGE.index(y), 1, i, row - ROWS] = 1.0
    return np.concatenate([own.reshape(128, -1), halo.reshape(128, -1)], axis=1).astype(BF16)


def spread_second():
    out = np.zeros((128, len(SLOTS), ROWS, CH), np.float32)
    for dy in range(5):
        for i in range(CH):
            for at, slot in enumerate(SLOTS):
                row = slot + dy - 2
                if 0 <= row < ROWS:
                    out[dy * CH + i, at, row, i] = 1.0
    return out.reshape(128, -1).astype(BF16)


def edge_rows():
    out = np.zeros((2, CH, 2, CH, ROWS), np.float32)
    for c in range(CH):
        for t in range(2):
            out[0, c, t, c, t] = 1.0
            out[1, c, t, c, ROWS - 2 + t] = 1.0
    return out.reshape(64, 128).astype(BF16)


def placed_rows():
    out = np.zeros((16, CH, CH, ROWS), np.float32)
    for c in range(CH):
        for y in range(ROWS):
            out[y, c, c, y] = 1.0
    return out.reshape(256, 128).astype(BF16)


def nt(a, b):
    return lax.dot_general(a, b, (((1,), (1,)), ((), ())), preferred_element_type=F32)


def gelu(x):
    return 0.5 * x * (1.0 + lax.erf(x * math.sqrt(0.5)))


def swap_blocks(x):
    sub = lax.broadcasted_iota(jnp.int32, x.shape, 1)
    block = lax.broadcasted_iota(jnp.int32, x.shape, 2) // CH
    for bit in (1, 2, 4):
        high_sub = (sub & bit) != 0
        high_block = (block & bit) != 0
        lane = CH * bit
        down = pltpu.roll(pltpu.roll(x, 8 - bit, 1), lane, 2)
        up = pltpu.roll(pltpu.roll(x, bit, 1), 128 - lane, 2)
        x = jnp.where(high_sub == high_block, x, jnp.where(high_sub, up, down))
    return x


def base_of(weight):
    pieces = [weight[dy].reshape(5 * CH, CH).astype(F32) for dy in range(5)]
    pieces.append(jnp.zeros((5 * CH, 128 - 5 * CH), F32))
    return jnp.concatenate(pieces, axis=1).astype(BF16)


def peers(me):
    z, x, core = me // 8, (me // 2) % 4, me % 2
    depths = [(3, 3 - z), (2, (z + 2) % 4), (1, (z // 2) * 2 + 1 - z % 2), (0, z)]
    widths = [(2, (x + 2) % 4), (1, (x + 1) % 4), (1, (x + 3) % 4), (0, x)]
    pairs = sorted(
        ((far + wide, far, n, depth, width)
         for far, depth in depths
         for n, (wide, width) in enumerate(widths)),
        key=lambda pair: (-pair[0], -pair[1], pair[2]),
    )
    found = []
    for total, _, _, depth, width in pairs:
        for twin in (1 - core, core):
            if total > 0 or twin is not core:
                found.append((depth * 4 + width) * 2 + twin)
    return found


def kernel(
    atm, w1, bias, w2, edge, spread1, spread2, placed, fourier, phase, table, result,
    shifted, halo, w1_v, bias_v, w2_v, edge_v, spread1_v, spread2_v, fourier_v, phase_v, table_v,
    t1, t1h, t2, hsend, acc, hidden, mixed, packed, received,
    load_sem, halo_send, halo_recv, a2a_send, a2a_recv,
):
    me = lax.axis_index("lat")
    barrier = pltpu.get_barrier_semaphore()

    loads = [
        (atm, shifted.at[pl.ds(256, 128), :]),
        (edge, edge_v),
        (w1, w1_v),
        (spread1, spread1_v),
        (bias, bias_v),
        (w2, w2_v),
        (spread2, spread2_v),
        (fourier, fourier_v),
        (placed, t2.at[:, pl.ds(640, 128)]),
        (phase, phase_v),
        (table.at[me], table_v),
    ]
    copies = [
        pltpu.make_async_copy(source, target, load_sem.at[n])
        for n, (source, target) in enumerate(loads)
    ]
    for copy in copies:
        copy.start()

    others = peers(me)
    for other in [lax.rem(me + 1, BANDS), lax.rem(me + BANDS - 1, BANDS)]:
        pl.semaphore_signal(
            barrier, inc=1, device_id={"lat": other}, device_id_type=pl.DeviceIdType.MESH
        )

    def greet(j, carry):
        pl.semaphore_signal(
            barrier, inc=1, device_id={"lat": lax.rem(me + j, BANDS)},
            device_id_type=pl.DeviceIdType.MESH,
        )
        return carry

    lax.fori_loop(2, BANDS - 1, greet, 0)

    copies[0].wait()
    copies[1].wait()
    hsend[...] = jnp.dot(
        edge_v[...], shifted[256:384, :], preferred_element_type=F32
    ).astype(BF16)

    pl.semaphore_wait(barrier, BANDS - 1)

    up = lax.max(me - 1, 0)
    down = lax.min(me + 1, BANDS - 1)
    to_up = pltpu.make_async_remote_copy(
        src_ref=hsend.at[pl.ds(0, 32), :], dst_ref=halo.at[pl.ds(160, 32), :],
        send_sem=halo_send.at[0], recv_sem=halo_recv.at[0],
        device_id={"lat": up}, device_id_type=pl.DeviceIdType.MESH,
    )
    to_down = pltpu.make_async_remote_copy(
        src_ref=hsend.at[pl.ds(32, 32), :], dst_ref=halo.at[pl.ds(128, 32), :],
        send_sem=halo_send.at[1], recv_sem=halo_recv.at[1],
        device_id={"lat": down}, device_id_type=pl.DeviceIdType.MESH,
    )

    @pl.when(me > 0)
    def _():
        to_up.start()

    @pl.when(me < BANDS - 1)
    def _():
        to_down.start()

    copies[2].wait()
    copies[3].wait()
    res1 = jnp.dot(base_of(w1_v), spread1_v[...], preferred_element_type=F32).astype(BF16)
    for dx in range(5):
        for y in range(ROWS):
            t1[16 * y : 16 * y + 16, 128 * dx : 128 * dx + 128] = res1[
                16 * dx : 16 * dx + 16, 128 * y : 128 * y + 128
            ]
        for e in range(4):
            t1h[16 * e : 16 * e + 16, 64 * dx : 64 * dx + 64] = res1[
                16 * dx : 16 * dx + 16, 1024 + 64 * e : 1088 + 64 * e
            ]

    own = shifted[256:384, :].astype(F32)
    for dx in (0, 1, 3, 4):
        shifted[128 * dx : 128 * dx + 128, :] = pltpu.roll(own, (2 - dx) % LON, 1).astype(BF16)
    copies[4].wait()
    eye = lax.broadcasted_iota(jnp.int32, (CH, CH), 0) == lax.broadcasted_iota(
        jnp.int32, (CH, CH), 1
    )
    column = jnp.sum(
        jnp.where(eye, jnp.broadcast_to(bias_v[...], (CH, CH)), 0.0), axis=1, keepdims=True
    )
    offsets = jnp.concatenate([column] * ROWS, axis=0)
    acc[...] = jnp.dot(t1[...], shifted[...], preferred_element_type=F32) + offsets
    hidden[32:96, :] = gelu(acc[32:96, :]).astype(BF16)

    copies[5].wait()
    copies[6].wait()
    res2 = jnp.dot(base_of(w2_v), spread2_v[...], preferred_element_type=F32).astype(BF16)
    for at, slot in enumerate(SLOTS):
        row = 16 * (slot % 16)
        for dx in range(5):
            t2[row : row + 16, 128 * dx : 128 * dx + 128] = res2[
                16 * dx : 16 * dx + 16, 128 * at : 128 * at + 128
            ]
    t2[160:224, 0:640] = jnp.zeros((64, 640), BF16)
    copies[7].wait()
    mixed[:, 640:768] = nt(fourier_v[...], shifted[256:384, :]).astype(BF16)

    @pl.when(me > 0)
    def _():
        to_up.wait_send()
        to_down.wait_recv()

    @pl.when(me < BANDS - 1)
    def _():
        to_down.wait_send()
        to_up.wait_recv()

    @pl.when(me == 0)
    def _():
        halo[128:160, :] = jnp.zeros((32, LON), BF16)

    @pl.when(me == BANDS - 1)
    def _():
        halo[160:192, :] = jnp.zeros((32, LON), BF16)

    rim = halo[128:192, :].astype(F32)
    for dx in (0, 1, 3, 4):
        halo[64 * dx : 64 * dx + 64, :] = pltpu.roll(rim, (2 - dx) % LON, 1).astype(BF16)
    more = jnp.dot(t1h[...], halo[...], preferred_element_type=F32)
    hidden[0:32, :] = gelu(acc[0:32, :] + more[0:32]).astype(BF16)
    hidden[96:128, :] = gelu(acc[96:128, :] + more[32:64]).astype(BF16)

    spectra = nt(fourier_v[...], hidden[...])
    swapped = pltpu.roll(spectra.reshape(BANDS, 8, 128), 4, 1).reshape(256, 128)
    copies[9].wait()
    mixed[:, 256:384] = spectra.astype(BF16)
    for step, low, high in ((1, 1, 3), (2, 0, 4)):
        straight = phase_v[2 * step - 2] * spectra
        crossed = phase_v[2 * step - 1] * swapped
        mixed[:, 128 * high : 128 * high + 128] = (straight + crossed).astype(BF16)
        mixed[:, 128 * low : 128 * low + 128] = (straight - crossed).astype(BF16)

    copies[8].wait()
    sums = nt(mixed[...], t2[...]).reshape(BANDS, 8, 256)
    near = swap_blocks(sums[:, :, 0:128])
    far = swap_blocks(sums[:, :, 128:256])
    packed[...] = jnp.concatenate([near, far], axis=1).astype(BF16)

    for p in others:
        pltpu.make_async_remote_copy(
            src_ref=packed.at[p], dst_ref=received.at[me],
            send_sem=a2a_send, recv_sem=a2a_recv,
            device_id={"lat": p}, device_id_type=pl.DeviceIdType.MESH,
        ).start()
    received[me] = packed[me]
    copies[10].wait()
    some = pltpu.make_async_remote_copy(
        src_ref=packed.at[pl.ds(0, BANDS - 1)], dst_ref=received.at[pl.ds(0, BANDS - 1)],
        send_sem=a2a_send, recv_sem=a2a_recv,
        device_id={"lat": lax.rem(me + 1, BANDS)}, device_id_type=pl.DeviceIdType.MESH,
    )
    some.wait_recv()

    parts = received[...].astype(F32)
    near = parts[:, 0:8, :]
    far = parts[:, 8:16, :]
    none = jnp.zeros((1, 8, 128), F32)
    above = jnp.concatenate([none, far[:-1]], axis=0)
    below = jnp.concatenate([far[1:], none], axis=0)
    first = lax.broadcasted_iota(jnp.int32, near.shape, 1) < 4
    rows = (near + jnp.where(first, above, below)).reshape(LAT, 128)
    lines = rows.T.astype(BF16)
    for m in range(OWN):
        left = jnp.concatenate([lines[16 * m : 16 * m + 16], lines[64 + 16 * m : 80 + 16 * m]], axis=0)
        done = jnp.dot(left, table_v[m], preferred_element_type=F32)
        for q in range(2):
            for a in range(2):
                result[m, q, pl.ds(a, CH, stride=2), :] = done[
                    16 * a : 16 * a + 16, 128 * q : 128 * q + 128
                ]
    some.wait_send()


def store(source, target, semaphore):
    copy = pltpu.make_async_copy(source, target, semaphore)
    copy.start()
    copy.wait()


@functools.cache
def constants():
    return (
        edge_rows(), spread_first(), spread_second(), placed_rows(), fourier_rows(),
        phase_rows(), projection_table(),
    )


def per_device(atmosphere, first_weight, first_bias, second_weight):
    edge, spread1, spread2, placed, fourier, phase, table = constants()
    operands = (
        atmosphere.reshape(CH * ROWS, LON),
        first_weight.transpose(2, 3, 0, 1),
        first_bias.reshape(1, CH),
        second_weight.transpose(2, 3, 0, 1),
        edge, spread1, spread2, placed, fourier, phase, table,
    )
    scratch = [
        pltpu.VMEM((640, LON), BF16),
        pltpu.VMEM((320, LON), BF16),
        pltpu.VMEM((5, 5, CH, CH), BF16),
        pltpu.VMEM((1, CH), F32),
        pltpu.VMEM((5, 5, CH, CH), BF16),
        pltpu.VMEM(edge.shape, BF16),
        pltpu.VMEM(spread1.shape, BF16),
        pltpu.VMEM(spread2.shape, BF16),
        pltpu.VMEM(fourier.shape, BF16),
        pltpu.VMEM(phase.shape, F32),
        pltpu.VMEM(table.shape[1:], BF16),
        pltpu.VMEM((128, 640), BF16),
        pltpu.VMEM((64, 320), BF16),
        pltpu.VMEM((256, 768), BF16),
        pltpu.VMEM((64, LON), BF16),
        pltpu.VMEM((128, LON), F32),
        pltpu.VMEM((128, LON), BF16),
        pltpu.VMEM((256, 768), BF16),
        pltpu.VMEM((BANDS, 16, 128), BF16),
        pltpu.VMEM((BANDS, 16, 128), BF16),
        pltpu.SemaphoreType.DMA((11,)),
        pltpu.SemaphoreType.DMA((2,)),
        pltpu.SemaphoreType.DMA((2,)),
        pltpu.SemaphoreType.DMA,
        pltpu.SemaphoreType.DMA,
    ]
    spectrum = pl.pallas_call(
        kernel,
        out_shape=jax.ShapeDtypeStruct((OWN, 2, 2 * CH, 128), F32),
        in_specs=[pl.BlockSpec(memory_space=pltpu.HBM)] * len(operands),
        out_specs=pl.BlockSpec(memory_space=pltpu.VMEM),
        scratch_shapes=scratch,
        compiler_params=pltpu.CompilerParams(
            collective_id=0, has_side_effects=True, vmem_limit_bytes=44 * 1024 * 1024
        ),
        name="encoder",
    )(*operands)
    spectrum = pl.pallas_call(
        store,
        out_shape=jax.ShapeDtypeStruct((OWN, 2, 2 * CH, 128), F32),
        in_specs=[pl.BlockSpec(memory_space=pltpu.VMEM)],
        out_specs=pl.BlockSpec(memory_space=pltpu.HBM),
        scratch_shapes=[pltpu.SemaphoreType.DMA],
        name="store",
    )(spectrum)
    return spectrum.reshape(OWN, 2, CH, 2, 128)


def solution(mesh):
    placed = (
        P("chan", "lat", None),
        P("chan", None, None, None),
        P("chan"),
        P("chan", None, None, None),
    )
    return jax.shard_map(
        per_device,
        mesh=mesh,
        in_specs=placed,
        out_specs=P("lat", None, "chan", None, None),
        check_vma=False,
    )
```

```python
import functools
import math

import jax
import jax.numpy as jnp
import numpy as np
from jax import lax
from jax.experimental import pallas as pl
from jax.experimental.pallas import tpu as pltpu
from jax.sharding import PartitionSpec as P

ORDERS = 128
DEGREES = 256
LAT = 256
LON = 1536
BANDS = 32
ROWS = 8
CH = 16
OWN = ORDERS // BANDS
BF16 = jnp.bfloat16
F32 = jnp.float32


def fourier_rows():
    orders = np.arange(1, ORDERS + 1)
    places = np.arange(LON)
    phases = (orders[:, None] * places[None, :] % LON) * (2.0 * math.pi / LON)
    real = np.cos(phases) / math.sqrt(LON)
    imag = -np.sin(phases) / math.sqrt(LON)
    both = np.stack([real.reshape(BANDS, OWN, LON), imag.reshape(BANDS, OWN, LON)], axis=1)
    return both.reshape(2 * ORDERS, LON).astype(BF16)


def phase_rows():
    orders = np.arange(1, ORDERS + 1).reshape(BANDS, OWN)
    out = []
    for step in (1, 2):
        angle = 2.0 * math.pi * step * orders / LON
        cosine = np.stack([np.cos(angle), np.cos(angle)], axis=1).reshape(2 * ORDERS)
        sine = np.stack([-np.sin(angle), np.sin(angle)], axis=1).reshape(2 * ORDERS)
        out += [cosine, sine]
    table = np.stack(out)[:, :, None]
    return np.broadcast_to(table, (4, 2 * ORDERS, 128)).astype(np.float32).copy()


def projection_table():
    half = LAT // 2
    single = np.float32
    theta = (math.pi * (np.arange(half) + 0.5) / LAT).astype(single)
    cosine, sine = np.cos(theta)[None, :], np.sin(theta)[None, :]
    order = np.arange(1, ORDERS + 1, dtype=single)[:, None]
    gamma = np.vectorize(math.lgamma, otypes=[single])
    log_diag = (
        single(0.5)
        * (
            np.log((2 * order + 1) / 2)
            + gamma(2 * order + 1)
            - order * single(math.log(4.0))
            - 2 * gamma(order + 1)
        )
        + order * np.log(sine)
    )

    def normal(value):
        return np.where(np.abs(value) < np.finfo(single).tiny, single(0.0), value)

    diagonal = normal(np.exp(log_diag))
    latest = np.zeros_like(diagonal)
    before = np.zeros_like(diagonal)
    stacked = np.zeros((DEGREES, ORDERS, half), single)
    for degree in range(DEGREES):
        real = single(degree)
        spread = np.maximum(real * real - order * order, single(1.0))
        raising = np.sqrt(np.maximum(4 * real * real - 1, single(1.0)) / spread)
        previous = real - 1
        lowering = np.sqrt(
            np.maximum(previous * previous - order * order, single(0.0))
            / np.maximum(4 * previous * previous - 1, single(1.0))
        )
        raised = normal(
            raising * normal(normal(cosine * latest) - normal(lowering * before))
        )
        result = np.where(order == real, diagonal, np.where(order < real, raised, single(0.0)))
        stacked[degree] = result
        latest, before = result, latest
    weighted = stacked * (single(math.pi) * sine / single(math.sqrt(LAT)))[None]
    weighted = weighted.astype(BF16).astype(single)
    degrees = np.arange(DEGREES)[:, None, None]
    numbers = np.arange(1, ORDERS + 1)[None, :, None]
    sign = np.where((degrees + numbers) % 2 == 0, 1.0, -1.0).astype(np.float32)
    whole = np.concatenate([weighted, (weighted * sign)[:, :, ::-1]], axis=2)
    whole = whole.reshape(DEGREES // 2, 2, ORDERS, LAT).transpose(2, 3, 1, 0)
    return whole.reshape(BANDS, OWN, LAT, DEGREES).astype(BF16)


EDGE = (0, 1, 6, 7)
SLOTS = (0, 1, 2, 3, 4, 5, 6, 7, 8, 9, -2, -1)


def spread_first():
    own = np.zeros((128, ROWS, CH, ROWS), np.float32)
    halo = np.zeros((128, 4, 2, CH, 2), np.float32)
    for dy in range(5):
        for i in range(CH):
            for y in range(ROWS):
                row = y + dy - 2
                if 0 <= row < ROWS:
                    own[dy * CH + i, y, i, row] = 1.0
                elif row < 0:
                    halo[dy * CH + i, EDGE.index(y), 0, i, row + 2] = 1.0
                else:
                    halo[dy * CH + i, EDGE.index(y), 1, i, row - ROWS] = 1.0
    return np.concatenate([own.reshape(128, -1), halo.reshape(128, -1)], axis=1).astype(BF16)


def spread_second():
    out = np.zeros((128, len(SLOTS), ROWS, CH), np.float32)
    for dy in range(5):
        for i in range(CH):
            for at, slot in enumerate(SLOTS):
                row = slot + dy - 2
                if 0 <= row < ROWS:
                    out[dy * CH + i, at, row, i] = 1.0
    return out.reshape(128, -1).astype(BF16)


def edge_rows():
    out = np.zeros((2, CH, 2, CH, ROWS), np.float32)
    for c in range(CH):
        for t in range(2):
            out[0, c, t, c, t] = 1.0
            out[1, c, t, c, ROWS - 2 + t] = 1.0
    return out.reshape(64, 128).astype(BF16)


def placed_rows():
    out = np.zeros((16, CH, CH, ROWS), np.float32)
    for c in range(CH):
        for y in range(ROWS):
            out[y, c, c, y] = 1.0
    return out.reshape(256, 128).astype(BF16)


def nt(a, b):
    return lax.dot_general(a, b, (((1,), (1,)), ((), ())), preferred_element_type=F32)


def gelu(x):
    return 0.5 * x * (1.0 + lax.erf(x * math.sqrt(0.5)))


def swap_blocks(x):
    sub = lax.broadcasted_iota(jnp.int32, x.shape, 1)
    block = lax.broadcasted_iota(jnp.int32, x.shape, 2) // CH
    for bit in (1, 2, 4):
        high_sub = (sub & bit) != 0
        high_block = (block & bit) != 0
        lane = CH * bit
        down = pltpu.roll(pltpu.roll(x, 8 - bit, 1), lane, 2)
        up = pltpu.roll(pltpu.roll(x, bit, 1), 128 - lane, 2)
        x = jnp.where(high_sub == high_block, x, jnp.where(high_sub, up, down))
    return x


def base_of(weight):
    pieces = [weight[dy].reshape(5 * CH, CH).astype(F32) for dy in range(5)]
    pieces.append(jnp.zeros((5 * CH, 128 - 5 * CH), F32))
    return jnp.concatenate(pieces, axis=1).astype(BF16)


def peers(me):
    z, x, core = me // 8, (me // 2) % 4, me % 2
    depths = [(3, 3 - z), (2, (z + 2) % 4), (1, (z // 2) * 2 + 1 - z % 2), (0, z)]
    widths = [(2, (x + 2) % 4), (1, (x + 1) % 4), (1, (x + 3) % 4), (0, x)]
    pairs = sorted(
        ((far + wide, far, n, depth, width)
         for far, depth in depths
         for n, (wide, width) in enumerate(widths)),
        key=lambda pair: (-pair[0], -pair[1], pair[2]),
    )
    found = []
    for total, _, _, depth, width in pairs:
        for twin in (1 - core, core):
            if total > 0 or twin is not core:
                found.append((depth * 4 + width) * 2 + twin)
    return found


def kernel(
    atm, w1, bias, w2, edge, spread1, spread2, placed, fourier, phase, table, result,
    shifted, halo, w1_v, bias_v, w2_v, edge_v, spread1_v, spread2_v, fourier_v, phase_v, table_v,
    t1, t1h, t2, hsend, acc, hidden, mixed, packed, received,
    load_sem, halo_send, halo_recv, a2a_send, a2a_recv,
):
    me = lax.axis_index("lat")
    barrier = pltpu.get_barrier_semaphore()

    loads = [
        (atm, shifted.at[pl.ds(256, 128), :]),
        (edge, edge_v),
        (w1, w1_v),
        (spread1, spread1_v),
        (bias, bias_v),
        (w2, w2_v),
        (spread2, spread2_v),
        (fourier, fourier_v),
        (placed, t2.at[:, pl.ds(640, 128)]),
        (phase, phase_v),
        (table.at[me], table_v),
    ]
    copies = [
        pltpu.make_async_copy(source, target, load_sem.at[n])
        for n, (source, target) in enumerate(loads)
    ]
    for copy in copies:
        copy.start()

    others = peers(me)
    for other in [lax.rem(me + 1, BANDS), lax.rem(me + BANDS - 1, BANDS)]:
        pl.semaphore_signal(
            barrier, inc=1, device_id={"lat": other}, device_id_type=pl.DeviceIdType.MESH
        )

    def greet(j, carry):
        pl.semaphore_signal(
            barrier, inc=1, device_id={"lat": lax.rem(me + j, BANDS)},
            device_id_type=pl.DeviceIdType.MESH,
        )
        return carry

    lax.fori_loop(2, BANDS - 1, greet, 0)

    copies[0].wait()
    copies[1].wait()
    hsend[...] = jnp.dot(
        edge_v[...], shifted[256:384, :], preferred_element_type=F32
    ).astype(BF16)

    pl.semaphore_wait(barrier, BANDS - 1)

    up = lax.max(me - 1, 0)
    down = lax.min(me + 1, BANDS - 1)
    to_up = pltpu.make_async_remote_copy(
        src_ref=hsend.at[pl.ds(0, 32), :], dst_ref=halo.at[pl.ds(160, 32), :],
        send_sem=halo_send.at[0], recv_sem=halo_recv.at[0],
        device_id={"lat": up}, device_id_type=pl.DeviceIdType.MESH,
    )
    to_down = pltpu.make_async_remote_copy(
        src_ref=hsend.at[pl.ds(32, 32), :], dst_ref=halo.at[pl.ds(128, 32), :],
        send_sem=halo_send.at[1], recv_sem=halo_recv.at[1],
        device_id={"lat": down}, device_id_type=pl.DeviceIdType.MESH,
    )

    @pl.when(me > 0)
    def _():
        to_up.start()

    @pl.when(me < BANDS - 1)
    def _():
        to_down.start()

    copies[2].wait()
    copies[3].wait()
    res1 = jnp.dot(base_of(w1_v), spread1_v[...], preferred_element_type=F32).astype(BF16)
    for dx in range(5):
        for y in range(ROWS):
            t1[16 * y : 16 * y + 16, 128 * dx : 128 * dx + 128] = res1[
                16 * dx : 16 * dx + 16, 128 * y : 128 * y + 128
            ]
        for e in range(4):
            t1h[16 * e : 16 * e + 16, 64 * dx : 64 * dx + 64] = res1[
                16 * dx : 16 * dx + 16, 1024 + 64 * e : 1088 + 64 * e
            ]

    own = shifted[256:384, :].astype(F32)
    for dx in (0, 1, 3, 4):
        shifted[128 * dx : 128 * dx + 128, :] = pltpu.roll(own, (2 - dx) % LON, 1).astype(BF16)
    copies[4].wait()
    eye = lax.broadcasted_iota(jnp.int32, (CH, CH), 0) == lax.broadcasted_iota(
        jnp.int32, (CH, CH), 1
    )
    column = jnp.sum(
        jnp.where(eye, jnp.broadcast_to(bias_v[...], (CH, CH)), 0.0), axis=1, keepdims=True
    )
    offsets = jnp.concatenate([column] * ROWS, axis=0)
    acc[...] = jnp.dot(t1[...], shifted[...], preferred_element_type=F32) + offsets
    hidden[32:96, :] = gelu(acc[32:96, :]).astype(BF16)

    copies[5].wait()
    copies[6].wait()
    res2 = jnp.dot(base_of(w2_v), spread2_v[...], preferred_element_type=F32).astype(BF16)
    for at, slot in enumerate(SLOTS):
        row = 16 * (slot % 16)
        for dx in range(5):
            t2[row : row + 16, 128 * dx : 128 * dx + 128] = res2[
                16 * dx : 16 * dx + 16, 128 * at : 128 * at + 128
            ]
    t2[160:224, 0:640] = jnp.zeros((64, 640), BF16)
    copies[7].wait()
    mixed[:, 640:768] = nt(fourier_v[...], shifted[256:384, :]).astype(BF16)

    @pl.when(me > 0)
    def _():
        to_up.wait_send()
        to_down.wait_recv()

    @pl.when(me < BANDS - 1)
    def _():
        to_down.wait_send()
        to_up.wait_recv()

    @pl.when(me == 0)
    def _():
        halo[128:160, :] = jnp.zeros((32, LON), BF16)

    @pl.when(me == BANDS - 1)
    def _():
        halo[160:192, :] = jnp.zeros((32, LON), BF16)

    rim = halo[128:192, :].astype(F32)
    for dx in (0, 1, 3, 4):
        halo[64 * dx : 64 * dx + 64, :] = pltpu.roll(rim, (2 - dx) % LON, 1).astype(BF16)
    more = jnp.dot(t1h[...], halo[...], preferred_element_type=F32)
    hidden[0:32, :] = gelu(acc[0:32, :] + more[0:32]).astype(BF16)
    hidden[96:128, :] = gelu(acc[96:128, :] + more[32:64]).astype(BF16)

    spectra = nt(fourier_v[...], hidden[...])
    swapped = pltpu.roll(spectra.reshape(BANDS, 8, 128), 4, 1).reshape(256, 128)
    copies[9].wait()
    mixed[:, 256:384] = spectra.astype(BF16)
    for step, low, high in ((1, 1, 3), (2, 0, 4)):
        straight = phase_v[2 * step - 2] * spectra
        crossed = phase_v[2 * step - 1] * swapped
        mixed[:, 128 * high : 128 * high + 128] = (straight + crossed).astype(BF16)
        mixed[:, 128 * low : 128 * low + 128] = (straight - crossed).astype(BF16)

    copies[8].wait()
    sums = nt(mixed[...], t2[...]).reshape(BANDS, 8, 256)
    near = swap_blocks(sums[:, :, 0:128])
    far = swap_blocks(sums[:, :, 128:256])
    packed[...] = jnp.concatenate([near, far], axis=1).astype(BF16)

    for p in others:
        pltpu.make_async_remote_copy(
            src_ref=packed.at[p], dst_ref=received.at[me],
            send_sem=a2a_send, recv_sem=a2a_recv,
            device_id={"lat": p}, device_id_type=pl.DeviceIdType.MESH,
        ).start()
    received[me] = packed[me]
    copies[10].wait()
    some = pltpu.make_async_remote_copy(
        src_ref=packed.at[pl.ds(0, BANDS - 1)], dst_ref=received.at[pl.ds(0, BANDS - 1)],
        send_sem=a2a_send, recv_sem=a2a_recv,
        device_id={"lat": lax.rem(me + 1, BANDS)}, device_id_type=pl.DeviceIdType.MESH,
    )
    some.wait_recv()

    parts = received[...].astype(F32)
    near = parts[:, 0:8, :]
    far = parts[:, 8:16, :]
    none = jnp.zeros((1, 8, 128), F32)
    above = jnp.concatenate([none, far[:-1]], axis=0)
    below = jnp.concatenate([far[1:], none], axis=0)
    first = lax.broadcasted_iota(jnp.int32, near.shape, 1) < 4
    rows = (near + jnp.where(first, above, below)).reshape(LAT, 128)
    lines = rows.T.astype(BF16)
    for m in range(OWN):
        left = jnp.concatenate([lines[16 * m : 16 * m + 16], lines[64 + 16 * m : 80 + 16 * m]], axis=0)
        done = jnp.dot(left, table_v[m], preferred_element_type=F32)
        for q in range(2):
            for a in range(2):
                result[m, q, pl.ds(a, CH, stride=2), :] = done[
                    16 * a : 16 * a + 16, 128 * q : 128 * q + 128
                ]
    some.wait_send()


def store(source, target, semaphore):
    copy = pltpu.make_async_copy(source, target, semaphore)
    copy.start()
    copy.wait()


@functools.cache
def constants():
    return (
        edge_rows(), spread_first(), spread_second(), placed_rows(), fourier_rows(),
        phase_rows(), projection_table(),
    )


def per_device(atmosphere, first_weight, first_bias, second_weight):
    edge, spread1, spread2, placed, fourier, phase, table = constants()
    operands = (
        atmosphere.reshape(CH * ROWS, LON),
        first_weight.transpose(2, 3, 0, 1),
        first_bias.reshape(1, CH),
        second_weight.transpose(2, 3, 0, 1),
        edge, spread1, spread2, placed, fourier, phase, table,
    )
    scratch = [
        pltpu.VMEM((640, LON), BF16),
        pltpu.VMEM((320, LON), BF16),
        pltpu.VMEM((5, 5, CH, CH), BF16),
        pltpu.VMEM((1, CH), F32),
        pltpu.VMEM((5, 5, CH, CH), BF16),
        pltpu.VMEM(edge.shape, BF16),
        pltpu.VMEM(spread1.shape, BF16),
        pltpu.VMEM(spread2.shape, BF16),
        pltpu.VMEM(fourier.shape, BF16),
        pltpu.VMEM(phase.shape, F32),
        pltpu.VMEM(table.shape[1:], BF16),
        pltpu.VMEM((128, 640), BF16),
        pltpu.VMEM((64, 320), BF16),
        pltpu.VMEM((256, 768), BF16),
        pltpu.VMEM((64, LON), BF16),
        pltpu.VMEM((128, LON), F32),
        pltpu.VMEM((128, LON), BF16),
        pltpu.VMEM((256, 768), BF16),
        pltpu.VMEM((BANDS, 16, 128), BF16),
        pltpu.VMEM((BANDS, 16, 128), BF16),
        pltpu.SemaphoreType.DMA((11,)),
        pltpu.SemaphoreType.DMA((2,)),
        pltpu.SemaphoreType.DMA((2,)),
        pltpu.SemaphoreType.DMA,
        pltpu.SemaphoreType.DMA,
    ]
    spectrum = pl.pallas_call(
        kernel,
        out_shape=pltpu.VMEM((OWN, 2, 2 * CH, 128), F32),
        in_specs=[pl.BlockSpec(memory_space=pltpu.HBM)] * len(operands),
        out_specs=pl.BlockSpec(memory_space=pltpu.VMEM),
        scratch_shapes=scratch,
        compiler_params=pltpu.CompilerParams(
            collective_id=0, has_side_effects=True, vmem_limit_bytes=56 * 1024 * 1024
        ),
        name="encoder",
    )(*operands)
    spectrum = pl.pallas_call(
        store,
        out_shape=jax.ShapeDtypeStruct((OWN, 2, 2 * CH, 128), F32),
        in_specs=[pl.BlockSpec(memory_space=pl.ANY)],
        compiler_params=pltpu.CompilerParams(vmem_limit_bytes=1024 * 1024),
        out_specs=pl.BlockSpec(memory_space=pltpu.HBM),
        scratch_shapes=[pltpu.SemaphoreType.DMA],
        name="store",
    )(spectrum)
    return spectrum.reshape(OWN, 2, CH, 2, 128)


def solution(mesh):
    placed = (
        P("chan", "lat", None),
        P("chan", None, None, None),
        P("chan"),
        P("chan", None, None, None),
    )
    return jax.shard_map(
        per_device,
        mesh=mesh,
        in_specs=placed,
        out_specs=P("lat", None, "chan", None, None),
        check_vma=False,
    )
```

```python
import functools
import math

import jax
import jax.numpy as jnp
import numpy as np
from jax import lax
from jax.experimental import pallas as pl
from jax.experimental.pallas import tpu as pltpu
from jax.sharding import PartitionSpec as P

ORDERS = 128
DEGREES = 256
LAT = 256
LON = 1536
BANDS = 32
ROWS = 8
CH = 16
OWN = ORDERS // BANDS
BF16 = jnp.bfloat16
F32 = jnp.float32


def fourier_rows():
    orders = np.arange(1, ORDERS + 1)
    places = np.arange(LON)
    phases = (orders[:, None] * places[None, :] % LON) * (2.0 * math.pi / LON)
    real = np.cos(phases) / math.sqrt(LON)
    imag = -np.sin(phases) / math.sqrt(LON)
    both = np.stack([real.reshape(BANDS, OWN, LON), imag.reshape(BANDS, OWN, LON)], axis=1)
    return both.reshape(2 * ORDERS, LON).astype(BF16)


def phase_rows():
    orders = np.arange(1, ORDERS + 1).reshape(BANDS, OWN)
    out = []
    for step in (1, 2):
        angle = 2.0 * math.pi * step * orders / LON
        cosine = np.stack([np.cos(angle), np.cos(angle)], axis=1).reshape(2 * ORDERS)
        sine = np.stack([-np.sin(angle), np.sin(angle)], axis=1).reshape(2 * ORDERS)
        out += [cosine, sine]
    table = np.stack(out)[:, :, None]
    return np.broadcast_to(table, (4, 2 * ORDERS, 128)).astype(np.float32).copy()


def projection_table():
    half = LAT // 2
    single = np.float32
    theta = (math.pi * (np.arange(half) + 0.5) / LAT).astype(single)
    cosine, sine = np.cos(theta)[None, :], np.sin(theta)[None, :]
    order = np.arange(1, ORDERS + 1, dtype=single)[:, None]
    gamma = np.vectorize(math.lgamma, otypes=[single])
    log_diag = (
        single(0.5)
        * (
            np.log((2 * order + 1) / 2)
            + gamma(2 * order + 1)
            - order * single(math.log(4.0))
            - 2 * gamma(order + 1)
        )
        + order * np.log(sine)
    )

    def normal(value):
        return np.where(np.abs(value) < np.finfo(single).tiny, single(0.0), value)

    diagonal = normal(np.exp(log_diag))
    latest = np.zeros_like(diagonal)
    before = np.zeros_like(diagonal)
    stacked = np.zeros((DEGREES, ORDERS, half), single)
    for degree in range(DEGREES):
        real = single(degree)
        spread = np.maximum(real * real - order * order, single(1.0))
        raising = np.sqrt(np.maximum(4 * real * real - 1, single(1.0)) / spread)
        previous = real - 1
        lowering = np.sqrt(
            np.maximum(previous * previous - order * order, single(0.0))
            / np.maximum(4 * previous * previous - 1, single(1.0))
        )
        raised = normal(
            raising * normal(normal(cosine * latest) - normal(lowering * before))
        )
        result = np.where(order == real, diagonal, np.where(order < real, raised, single(0.0)))
        stacked[degree] = result
        latest, before = result, latest
    weighted = stacked * (single(math.pi) * sine / single(math.sqrt(LAT)))[None]
    weighted = weighted.astype(BF16).astype(single)
    degrees = np.arange(DEGREES)[:, None, None]
    numbers = np.arange(1, ORDERS + 1)[None, :, None]
    sign = np.where((degrees + numbers) % 2 == 0, 1.0, -1.0).astype(np.float32)
    whole = np.concatenate([weighted, (weighted * sign)[:, :, ::-1]], axis=2)
    whole = whole.reshape(DEGREES // 2, 2, ORDERS, LAT).transpose(2, 3, 1, 0)
    return whole.reshape(BANDS, OWN, LAT, DEGREES).astype(BF16)


EDGE = (0, 1, 6, 7)
SLOTS = (0, 1, 2, 3, 4, 5, 6, 7, 8, 9, -2, -1)


def spread_first():
    own = np.zeros((128, ROWS, CH, ROWS), np.float32)
    halo = np.zeros((128, 4, 2, CH, 2), np.float32)
    for dy in range(5):
        for i in range(CH):
            for y in range(ROWS):
                row = y + dy - 2
                if 0 <= row < ROWS:
                    own[dy * CH + i, y, i, row] = 1.0
                elif row < 0:
                    halo[dy * CH + i, EDGE.index(y), 0, i, row + 2] = 1.0
                else:
                    halo[dy * CH + i, EDGE.index(y), 1, i, row - ROWS] = 1.0
    return np.concatenate([own.reshape(128, -1), halo.reshape(128, -1)], axis=1).astype(BF16)


def spread_second():
    out = np.zeros((128, len(SLOTS), ROWS, CH), np.float32)
    for dy in range(5):
        for i in range(CH):
            for at, slot in enumerate(SLOTS):
                row = slot + dy - 2
                if 0 <= row < ROWS:
                    out[dy * CH + i, at, row, i] = 1.0
    return out.reshape(128, -1).astype(BF16)


def edge_rows():
    out = np.zeros((2, CH, 2, CH, ROWS), np.float32)
    for c in range(CH):
        for t in range(2):
            out[0, c, t, c, t] = 1.0
            out[1, c, t, c, ROWS - 2 + t] = 1.0
    return out.reshape(64, 128).astype(BF16)


def placed_rows():
    out = np.zeros((16, CH, CH, ROWS), np.float32)
    for c in range(CH):
        for y in range(ROWS):
            out[y, c, c, y] = 1.0
    return out.reshape(256, 128).astype(BF16)


def nt(a, b):
    return lax.dot_general(a, b, (((1,), (1,)), ((), ())), preferred_element_type=F32)


def gelu(x):
    return 0.5 * x * (1.0 + lax.erf(x * math.sqrt(0.5)))


def swap_blocks(x):
    sub = lax.broadcasted_iota(jnp.int32, x.shape, 1)
    block = lax.broadcasted_iota(jnp.int32, x.shape, 2) // CH
    for bit in (1, 2, 4):
        high_sub = (sub & bit) != 0
        high_block = (block & bit) != 0
        lane = CH * bit
        down = pltpu.roll(pltpu.roll(x, 8 - bit, 1), lane, 2)
        up = pltpu.roll(pltpu.roll(x, bit, 1), 128 - lane, 2)
        x = jnp.where(high_sub == high_block, x, jnp.where(high_sub, up, down))
    return x


def base_of(weight):
    pieces = [weight[dy].reshape(5 * CH, CH).astype(F32) for dy in range(5)]
    pieces.append(jnp.zeros((5 * CH, 128 - 5 * CH), F32))
    return jnp.concatenate(pieces, axis=1).astype(BF16)


def peers(me):
    z, x, core = me // 8, (me // 2) % 4, me % 2
    depths = [(3, 3 - z), (2, (z + 2) % 4), (1, (z // 2) * 2 + 1 - z % 2), (0, z)]
    widths = [(2, (x + 2) % 4), (1, (x + 1) % 4), (1, (x + 3) % 4), (0, x)]
    pairs = sorted(
        ((far + wide, far, n, depth, width)
         for far, depth in depths
         for n, (wide, width) in enumerate(widths)),
        key=lambda pair: (-pair[0], -pair[1], pair[2]),
    )
    found = []
    for total, _, _, depth, width in pairs:
        for twin in (1 - core, core):
            if total > 0 or twin is not core:
                found.append((depth * 4 + width) * 2 + twin)
    return found


def kernel(
    atm, w1, bias, w2, edge, spread1, spread2, placed, fourier, phase, table, result,
    shifted, halo, w1_v, bias_v, w2_v, edge_v, spread1_v, spread2_v, fourier_v, phase_v, table_v,
    t1, t1h, t2, hsend, acc, hidden, mixed, packed, received,
    load_sem, halo_send, halo_recv, a2a_send, a2a_recv, rows_in,
):
    me = lax.axis_index("lat")
    barrier = pltpu.get_barrier_semaphore()

    loads = [
        (atm, shifted.at[pl.ds(256, 128), :]),
        (edge, edge_v),
        (w1, w1_v),
        (spread1, spread1_v),
        (bias, bias_v),
        (w2, w2_v),
        (spread2, spread2_v),
        (fourier, fourier_v),
        (placed, t2.at[:, pl.ds(640, 128)]),
        (phase, phase_v),
        (table.at[me], table_v),
    ]
    copies = [
        pltpu.make_async_copy(source, target, load_sem.at[n])
        for n, (source, target) in enumerate(loads)
    ]
    for copy in copies:
        copy.start()

    others = peers(me)
    column, depth = me % 8, me // 8
    line = [8 * ((depth + k) % 4) + column for k in (1, 2, 3)]
    row = [8 * depth + (column + k) % 8 for k in (1, 7, 2, 6, 3, 5, 4)]

    def tell(semaphore, other):
        pl.semaphore_signal(
            semaphore, inc=1, device_id={"lat": other}, device_id_type=pl.DeviceIdType.MESH
        )

    step = jnp.where(column == 7, 1, -1)
    crossing = ((column == 7) & (me < BANDS - 1)) | ((column == 0) & (me > 0))

    @pl.when(crossing)
    def _():
        tell(barrier, me + step)

    for other in row + line:
        tell(barrier, other)

    copies[0].wait()
    copies[1].wait()
    hsend[...] = jnp.dot(
        edge_v[...], shifted[256:384, :], preferred_element_type=F32
    ).astype(BF16)

    pl.semaphore_wait(barrier, jnp.where(crossing, 11, 10))

    up = lax.max(me - 1, 0)
    down = lax.min(me + 1, BANDS - 1)
    to_up = pltpu.make_async_remote_copy(
        src_ref=hsend.at[pl.ds(0, 32), :], dst_ref=halo.at[pl.ds(160, 32), :],
        send_sem=halo_send.at[0], recv_sem=halo_recv.at[0],
        device_id={"lat": up}, device_id_type=pl.DeviceIdType.MESH,
    )
    to_down = pltpu.make_async_remote_copy(
        src_ref=hsend.at[pl.ds(32, 32), :], dst_ref=halo.at[pl.ds(128, 32), :],
        send_sem=halo_send.at[1], recv_sem=halo_recv.at[1],
        device_id={"lat": down}, device_id_type=pl.DeviceIdType.MESH,
    )

    @pl.when(me > 0)
    def _():
        to_up.start()

    @pl.when(me < BANDS - 1)
    def _():
        to_down.start()

    for other in line:
        tell(rows_in, other)

    copies[2].wait()
    copies[3].wait()
    res1 = jnp.dot(base_of(w1_v), spread1_v[...], preferred_element_type=F32).astype(BF16)
    for dx in range(5):
        for y in range(ROWS):
            t1[16 * y : 16 * y + 16, 128 * dx : 128 * dx + 128] = res1[
                16 * dx : 16 * dx + 16, 128 * y : 128 * y + 128
            ]
        for e in range(4):
            t1h[16 * e : 16 * e + 16, 64 * dx : 64 * dx + 64] = res1[
                16 * dx : 16 * dx + 16, 1024 + 64 * e : 1088 + 64 * e
            ]

    own = shifted[256:384, :].astype(F32)
    for dx in (0, 1, 3, 4):
        shifted[128 * dx : 128 * dx + 128, :] = pltpu.roll(own, (2 - dx) % LON, 1).astype(BF16)
    copies[4].wait()
    eye = lax.broadcasted_iota(jnp.int32, (CH, CH), 0) == lax.broadcasted_iota(
        jnp.int32, (CH, CH), 1
    )
    column = jnp.sum(
        jnp.where(eye, jnp.broadcast_to(bias_v[...], (CH, CH)), 0.0), axis=1, keepdims=True
    )
    offsets = jnp.concatenate([column] * ROWS, axis=0)
    acc[...] = jnp.dot(t1[...], shifted[...], preferred_element_type=F32) + offsets
    hidden[32:96, :] = gelu(acc[32:96, :]).astype(BF16)

    copies[5].wait()
    copies[6].wait()
    res2 = jnp.dot(base_of(w2_v), spread2_v[...], preferred_element_type=F32).astype(BF16)
    for at, slot in enumerate(SLOTS):
        row = 16 * (slot % 16)
        for dx in range(5):
            t2[row : row + 16, 128 * dx : 128 * dx + 128] = res2[
                16 * dx : 16 * dx + 16, 128 * at : 128 * at + 128
            ]
    t2[160:224, 0:640] = jnp.zeros((64, 640), BF16)
    copies[7].wait()
    mixed[:, 640:768] = nt(fourier_v[...], shifted[256:384, :]).astype(BF16)

    @pl.when(me > 0)
    def _():
        to_up.wait_send()
        to_down.wait_recv()

    @pl.when(me < BANDS - 1)
    def _():
        to_down.wait_send()
        to_up.wait_recv()

    @pl.when(me == 0)
    def _():
        halo[128:160, :] = jnp.zeros((32, LON), BF16)

    @pl.when(me == BANDS - 1)
    def _():
        halo[160:192, :] = jnp.zeros((32, LON), BF16)

    rim = halo[128:192, :].astype(F32)
    for dx in (0, 1, 3, 4):
        halo[64 * dx : 64 * dx + 64, :] = pltpu.roll(rim, (2 - dx) % LON, 1).astype(BF16)
    more = jnp.dot(t1h[...], halo[...], preferred_element_type=F32)
    hidden[0:32, :] = gelu(acc[0:32, :] + more[0:32]).astype(BF16)
    hidden[96:128, :] = gelu(acc[96:128, :] + more[32:64]).astype(BF16)

    spectra = nt(fourier_v[...], hidden[...])
    swapped = pltpu.roll(spectra.reshape(BANDS, 8, 128), 4, 1).reshape(256, 128)
    copies[9].wait()
    mixed[:, 256:384] = spectra.astype(BF16)
    for step, low, high in ((1, 1, 3), (2, 0, 4)):
        straight = phase_v[2 * step - 2] * spectra
        crossed = phase_v[2 * step - 1] * swapped
        mixed[:, 128 * high : 128 * high + 128] = (straight + crossed).astype(BF16)
        mixed[:, 128 * low : 128 * low + 128] = (straight - crossed).astype(BF16)

    copies[8].wait()
    sums = nt(mixed[...], t2[...]).reshape(BANDS, 8, 256)
    near = swap_blocks(sums[:, :, 0:128])
    far = swap_blocks(sums[:, :, 128:256])
    packed[...] = jnp.concatenate([near, far], axis=1).astype(BF16)

    pl.semaphore_wait(rows_in, 3)
    for p in others:
        pltpu.make_async_remote_copy(
            src_ref=packed.at[p], dst_ref=received.at[me],
            send_sem=a2a_send, recv_sem=a2a_recv,
            device_id={"lat": p}, device_id_type=pl.DeviceIdType.MESH,
        ).start()
    received[me] = packed[me]
    copies[10].wait()
    some = pltpu.make_async_remote_copy(
        src_ref=packed.at[pl.ds(0, BANDS - 1)], dst_ref=received.at[pl.ds(0, BANDS - 1)],
        send_sem=a2a_send, recv_sem=a2a_recv,
        device_id={"lat": lax.rem(me + 1, BANDS)}, device_id_type=pl.DeviceIdType.MESH,
    )
    some.wait_recv()

    parts = received[...].astype(F32)
    near = parts[:, 0:8, :]
    far = parts[:, 8:16, :]
    none = jnp.zeros((1, 8, 128), F32)
    above = jnp.concatenate([none, far[:-1]], axis=0)
    below = jnp.concatenate([far[1:], none], axis=0)
    first = lax.broadcasted_iota(jnp.int32, near.shape, 1) < 4
    rows = (near + jnp.where(first, above, below)).reshape(LAT, 128)
    lines = rows.T.astype(BF16)
    for m in range(OWN):
        left = jnp.concatenate([lines[16 * m : 16 * m + 16], lines[64 + 16 * m : 80 + 16 * m]], axis=0)
        done = jnp.dot(left, table_v[m], preferred_element_type=F32)
        for q in range(2):
            for a in range(2):
                result[m, q, pl.ds(a, CH, stride=2), :] = done[
                    16 * a : 16 * a + 16, 128 * q : 128 * q + 128
                ]
    some.wait_send()


def store(source, target, semaphore):
    copy = pltpu.make_async_copy(source, target, semaphore)
    copy.start()
    copy.wait()


@functools.cache
def constants():
    return (
        edge_rows(), spread_first(), spread_second(), placed_rows(), fourier_rows(),
        phase_rows(), projection_table(),
    )


def per_device(atmosphere, first_weight, first_bias, second_weight):
    edge, spread1, spread2, placed, fourier, phase, table = constants()
    operands = (
        atmosphere.reshape(CH * ROWS, LON),
        first_weight.transpose(2, 3, 0, 1),
        first_bias.reshape(1, CH),
        second_weight.transpose(2, 3, 0, 1),
        edge, spread1, spread2, placed, fourier, phase, table,
    )
    scratch = [
        pltpu.VMEM((640, LON), BF16),
        pltpu.VMEM((320, LON), BF16),
        pltpu.VMEM((5, 5, CH, CH), BF16),
        pltpu.VMEM((1, CH), F32),
        pltpu.VMEM((5, 5, CH, CH), BF16),
        pltpu.VMEM(edge.shape, BF16),
        pltpu.VMEM(spread1.shape, BF16),
        pltpu.VMEM(spread2.shape, BF16),
        pltpu.VMEM(fourier.shape, BF16),
        pltpu.VMEM(phase.shape, F32),
        pltpu.VMEM(table.shape[1:], BF16),
        pltpu.VMEM((128, 640), BF16),
        pltpu.VMEM((64, 320), BF16),
        pltpu.VMEM((256, 768), BF16),
        pltpu.VMEM((64, LON), BF16),
        pltpu.VMEM((128, LON), F32),
        pltpu.VMEM((128, LON), BF16),
        pltpu.VMEM((256, 768), BF16),
        pltpu.VMEM((BANDS, 16, 128), BF16),
        pltpu.VMEM((BANDS, 16, 128), BF16),
        pltpu.SemaphoreType.DMA((11,)),
        pltpu.SemaphoreType.DMA((2,)),
        pltpu.SemaphoreType.DMA((2,)),
        pltpu.SemaphoreType.DMA,
        pltpu.SemaphoreType.DMA,
        pltpu.SemaphoreType.REGULAR,
    ]
    spectrum = pl.pallas_call(
        kernel,
        out_shape=pltpu.VMEM((OWN, 2, 2 * CH, 128), F32),
        in_specs=[pl.BlockSpec(memory_space=pltpu.HBM)] * len(operands),
        out_specs=pl.BlockSpec(memory_space=pltpu.VMEM),
        scratch_shapes=scratch,
        compiler_params=pltpu.CompilerParams(
            collective_id=0, has_side_effects=True, vmem_limit_bytes=56 * 1024 * 1024
        ),
        name="encoder",
    )(*operands)
    spectrum = pl.pallas_call(
        store,
        out_shape=jax.ShapeDtypeStruct((OWN, 2, 2 * CH, 128), F32),
        in_specs=[pl.BlockSpec(memory_space=pl.ANY)],
        compiler_params=pltpu.CompilerParams(vmem_limit_bytes=1024 * 1024),
        out_specs=pl.BlockSpec(memory_space=pltpu.HBM),
        scratch_shapes=[pltpu.SemaphoreType.DMA],
        name="store",
    )(spectrum)
    return spectrum.reshape(OWN, 2, CH, 2, 128)


def solution(mesh):
    placed = (
        P("chan", "lat", None),
        P("chan", None, None, None),
        P("chan"),
        P("chan", None, None, None),
    )
    return jax.shard_map(
        per_device,
        mesh=mesh,
        in_specs=placed,
        out_specs=P("lat", None, "chan", None, None),
        check_vma=False,
    )
```

```python
import functools
import math

import jax
import jax.numpy as jnp
import numpy as np
from jax import lax
from jax.experimental import pallas as pl
from jax.experimental.pallas import tpu as pltpu
from jax.sharding import PartitionSpec as P

ORDERS = 128
DEGREES = 256
LAT = 256
LON = 1536
BANDS = 32
ROWS = 8
CH = 16
OWN = ORDERS // BANDS
BF16 = jnp.bfloat16
F32 = jnp.float32


def fourier_rows():
    orders = np.arange(1, ORDERS + 1)
    places = np.arange(LON)
    phases = (orders[:, None] * places[None, :] % LON) * (2.0 * math.pi / LON)
    real = np.cos(phases) / math.sqrt(LON)
    imag = -np.sin(phases) / math.sqrt(LON)
    both = np.stack([real.reshape(BANDS, OWN, LON), imag.reshape(BANDS, OWN, LON)], axis=1)
    return both.reshape(2 * ORDERS, LON).astype(BF16)


def phase_rows():
    orders = np.arange(1, ORDERS + 1).reshape(BANDS, OWN)
    out = []
    for step in (1, 2):
        angle = 2.0 * math.pi * step * orders / LON
        cosine = np.stack([np.cos(angle), np.cos(angle)], axis=1).reshape(2 * ORDERS)
        sine = np.stack([-np.sin(angle), np.sin(angle)], axis=1).reshape(2 * ORDERS)
        out += [cosine, sine]
    table = np.stack(out)[:, :, None]
    return np.broadcast_to(table, (4, 2 * ORDERS, 128)).astype(np.float32).copy()


def projection_table():
    half = LAT // 2
    single = np.float32
    theta = (math.pi * (np.arange(half) + 0.5) / LAT).astype(single)
    cosine, sine = np.cos(theta)[None, :], np.sin(theta)[None, :]
    order = np.arange(1, ORDERS + 1, dtype=single)[:, None]
    gamma = np.vectorize(math.lgamma, otypes=[single])
    log_diag = (
        single(0.5)
        * (
            np.log((2 * order + 1) / 2)
            + gamma(2 * order + 1)
            - order * single(math.log(4.0))
            - 2 * gamma(order + 1)
        )
        + order * np.log(sine)
    )

    def normal(value):
        return np.where(np.abs(value) < np.finfo(single).tiny, single(0.0), value)

    diagonal = normal(np.exp(log_diag))
    latest = np.zeros_like(diagonal)
    before = np.zeros_like(diagonal)
    stacked = np.zeros((DEGREES, ORDERS, half), single)
    for degree in range(DEGREES):
        real = single(degree)
        spread = np.maximum(real * real - order * order, single(1.0))
        raising = np.sqrt(np.maximum(4 * real * real - 1, single(1.0)) / spread)
        previous = real - 1
        lowering = np.sqrt(
            np.maximum(previous * previous - order * order, single(0.0))
            / np.maximum(4 * previous * previous - 1, single(1.0))
        )
        raised = normal(
            raising * normal(normal(cosine * latest) - normal(lowering * before))
        )
        result = np.where(order == real, diagonal, np.where(order < real, raised, single(0.0)))
        stacked[degree] = result
        latest, before = result, latest
    weighted = stacked * (single(math.pi) * sine / single(math.sqrt(LAT)))[None]
    weighted = weighted.astype(BF16).astype(single)
    degrees = np.arange(DEGREES)[:, None, None]
    numbers = np.arange(1, ORDERS + 1)[None, :, None]
    sign = np.where((degrees + numbers) % 2 == 0, 1.0, -1.0).astype(np.float32)
    whole = np.concatenate([weighted, (weighted * sign)[:, :, ::-1]], axis=2)
    whole = whole.reshape(DEGREES // 2, 2, ORDERS, LAT).transpose(2, 3, 1, 0)
    return whole.reshape(BANDS, OWN, LAT, DEGREES).astype(BF16)


EDGE = (0, 1, 6, 7)
SLOTS = (0, 1, 2, 3, 4, 5, 6, 7, 8, 9, -2, -1)


def spread_first():
    own = np.zeros((128, ROWS, CH, ROWS), np.float32)
    halo = np.zeros((128, 4, 2, CH, 2), np.float32)
    for dy in range(5):
        for i in range(CH):
            for y in range(ROWS):
                row = y + dy - 2
                if 0 <= row < ROWS:
                    own[dy * CH + i, y, i, row] = 1.0
                elif row < 0:
                    halo[dy * CH + i, EDGE.index(y), 0, i, row + 2] = 1.0
                else:
                    halo[dy * CH + i, EDGE.index(y), 1, i, row - ROWS] = 1.0
    return np.concatenate([own.reshape(128, -1), halo.reshape(128, -1)], axis=1).astype(BF16)


def spread_second():
    out = np.zeros((128, len(SLOTS), ROWS, CH), np.float32)
    for dy in range(5):
        for i in range(CH):
            for at, slot in enumerate(SLOTS):
                row = slot + dy - 2
                if 0 <= row < ROWS:
                    out[dy * CH + i, at, row, i] = 1.0
    return out.reshape(128, -1).astype(BF16)


def edge_rows():
    out = np.zeros((2, CH, 2, CH, ROWS), np.float32)
    for c in range(CH):
        for t in range(2):
            out[0, c, t, c, t] = 1.0
            out[1, c, t, c, ROWS - 2 + t] = 1.0
    return out.reshape(64, 128).astype(BF16)


def placed_rows():
    out = np.zeros((16, CH, CH, ROWS), np.float32)
    for c in range(CH):
        for y in range(ROWS):
            out[y, c, c, y] = 1.0
    return out.reshape(256, 128).astype(BF16)


def nt(a, b):
    return lax.dot_general(a, b, (((1,), (1,)), ((), ())), preferred_element_type=F32)


def gelu(x):
    return 0.5 * x * (1.0 + lax.erf(x * math.sqrt(0.5)))


def swap_blocks(x):
    sub = lax.broadcasted_iota(jnp.int32, x.shape, 1)
    block = lax.broadcasted_iota(jnp.int32, x.shape, 2) // CH
    for bit in (1, 2, 4):
        high_sub = (sub & bit) != 0
        high_block = (block & bit) != 0
        lane = CH * bit
        down = pltpu.roll(pltpu.roll(x, 8 - bit, 1), lane, 2)
        up = pltpu.roll(pltpu.roll(x, bit, 1), 128 - lane, 2)
        x = jnp.where(high_sub == high_block, x, jnp.where(high_sub, up, down))
    return x


def base_of(weight):
    pieces = [weight[dy].reshape(5 * CH, CH).astype(F32) for dy in range(5)]
    pieces.append(jnp.zeros((5 * CH, 128 - 5 * CH), F32))
    return jnp.concatenate(pieces, axis=1).astype(BF16)


def peers(me):
    z, x, core = me // 8, (me // 2) % 4, me % 2
    depths = [(3, 3 - z), (2, (z + 2) % 4), (1, (z // 2) * 2 + 1 - z % 2), (0, z)]
    widths = [(2, (x + 2) % 4), (1, (x + 1) % 4), (1, (x + 3) % 4), (0, x)]
    pairs = sorted(
        ((far + wide, far, n, depth, width)
         for far, depth in depths
         for n, (wide, width) in enumerate(widths)),
        key=lambda pair: (-pair[0], -pair[1], pair[2]),
    )
    found = []
    for total, _, _, depth, width in pairs:
        for twin in (1 - core, core):
            if total > 0 or twin is not core:
                found.append((depth * 4 + width) * 2 + twin)
    return found


def kernel(
    atm, w1, bias, w2, edge, spread1, spread2, placed, fourier, phase, table, result,
    shifted, halo, w1_v, bias_v, w2_v, edge_v, spread1_v, spread2_v, fourier_v, phase_v, table_v,
    t1, t1h, t2, hsend, acc, hidden, mixed, packed, received,
    load_sem, halo_send, halo_recv, a2a_send, a2a_recv, rows_in,
):
    me = lax.axis_index("lat")
    barrier = pltpu.get_barrier_semaphore()

    loads = [
        (atm, shifted.at[pl.ds(256, 128), :]),
        (edge, edge_v),
        (w1, w1_v),
        (spread1, spread1_v),
        (bias, bias_v),
        (w2, w2_v),
        (spread2, spread2_v),
        (fourier, fourier_v),
        (placed, t2.at[:, pl.ds(640, 128)]),
        (phase, phase_v),
        (table.at[me], table_v),
    ]
    copies = [
        pltpu.make_async_copy(source, target, load_sem.at[n])
        for n, (source, target) in enumerate(loads)
    ]
    copies[0].start()
    copies[1].start()
    others = peers(me)
    column, depth = me % 8, me // 8
    line = [8 * ((depth + k) % 4) + column for k in (1, 2, 3)]
    row = [8 * depth + (column + k) % 8 for k in (1, 7, 2, 6, 3, 5, 4)]

    def tell(semaphore, other):
        pl.semaphore_signal(
            semaphore, inc=1, device_id={"lat": other}, device_id_type=pl.DeviceIdType.MESH
        )

    step = jnp.where(column == 7, 1, -1)
    crossing = ((column == 7) & (me < BANDS - 1)) | ((column == 0) & (me > 0))

    @pl.when(crossing)
    def _():
        tell(barrier, me + step)

    for other in row + line:
        tell(barrier, other)

    for copy in copies[2:]:
        copy.start()

    copies[0].wait()
    copies[1].wait()
    hsend[...] = jnp.dot(
        edge_v[...], shifted[256:384, :], preferred_element_type=F32
    ).astype(BF16)

    pl.semaphore_wait(barrier, jnp.where(crossing, 11, 10))

    up = lax.max(me - 1, 0)
    down = lax.min(me + 1, BANDS - 1)
    to_up = pltpu.make_async_remote_copy(
        src_ref=hsend.at[pl.ds(0, 32), :], dst_ref=halo.at[pl.ds(160, 32), :],
        send_sem=halo_send.at[0], recv_sem=halo_recv.at[0],
        device_id={"lat": up}, device_id_type=pl.DeviceIdType.MESH,
    )
    to_down = pltpu.make_async_remote_copy(
        src_ref=hsend.at[pl.ds(32, 32), :], dst_ref=halo.at[pl.ds(128, 32), :],
        send_sem=halo_send.at[1], recv_sem=halo_recv.at[1],
        device_id={"lat": down}, device_id_type=pl.DeviceIdType.MESH,
    )

    @pl.when(me > 0)
    def _():
        to_up.start()

    @pl.when(me < BANDS - 1)
    def _():
        to_down.start()

    for other in line:
        tell(rows_in, other)

    copies[2].wait()
    copies[3].wait()
    res1 = jnp.dot(base_of(w1_v), spread1_v[...], preferred_element_type=F32).astype(BF16)
    for dx in range(5):
        for y in range(ROWS):
            t1[16 * y : 16 * y + 16, 128 * dx : 128 * dx + 128] = res1[
                16 * dx : 16 * dx + 16, 128 * y : 128 * y + 128
            ]
        for e in range(4):
            t1h[16 * e : 16 * e + 16, 64 * dx : 64 * dx + 64] = res1[
                16 * dx : 16 * dx + 16, 1024 + 64 * e : 1088 + 64 * e
            ]

    own = shifted[256:384, :].astype(F32)
    for dx in (0, 1, 3, 4):
        shifted[128 * dx : 128 * dx + 128, :] = pltpu.roll(own, (2 - dx) % LON, 1).astype(BF16)
    copies[4].wait()
    eye = lax.broadcasted_iota(jnp.int32, (CH, CH), 0) == lax.broadcasted_iota(
        jnp.int32, (CH, CH), 1
    )
    column = jnp.sum(
        jnp.where(eye, jnp.broadcast_to(bias_v[...], (CH, CH)), 0.0), axis=1, keepdims=True
    )
    offsets = jnp.concatenate([column] * ROWS, axis=0)
    acc[...] = jnp.dot(t1[...], shifted[...], preferred_element_type=F32) + offsets
    hidden[32:96, :] = gelu(acc[32:96, :]).astype(BF16)

    copies[5].wait()
    copies[6].wait()
    res2 = jnp.dot(base_of(w2_v), spread2_v[...], preferred_element_type=F32).astype(BF16)
    for at, slot in enumerate(SLOTS):
        row = 16 * (slot % 16)
        for dx in range(5):
            t2[row : row + 16, 128 * dx : 128 * dx + 128] = res2[
                16 * dx : 16 * dx + 16, 128 * at : 128 * at + 128
            ]
    t2[160:224, 0:640] = jnp.zeros((64, 640), BF16)
    copies[7].wait()
    mixed[:, 640:768] = nt(fourier_v[...], shifted[256:384, :]).astype(BF16)

    @pl.when(me > 0)
    def _():
        to_up.wait_send()
        to_down.wait_recv()

    @pl.when(me < BANDS - 1)
    def _():
        to_down.wait_send()
        to_up.wait_recv()

    @pl.when(me == 0)
    def _():
        halo[128:160, :] = jnp.zeros((32, LON), BF16)

    @pl.when(me == BANDS - 1)
    def _():
        halo[160:192, :] = jnp.zeros((32, LON), BF16)

    rim = halo[128:192, :].astype(F32)
    for dx in (0, 1, 3, 4):
        halo[64 * dx : 64 * dx + 64, :] = pltpu.roll(rim, (2 - dx) % LON, 1).astype(BF16)
    more = jnp.dot(t1h[...], halo[...], preferred_element_type=F32)
    hidden[0:32, :] = gelu(acc[0:32, :] + more[0:32]).astype(BF16)
    hidden[96:128, :] = gelu(acc[96:128, :] + more[32:64]).astype(BF16)

    spectra = nt(fourier_v[...], hidden[...])
    swapped = pltpu.roll(spectra.reshape(BANDS, 8, 128), 4, 1).reshape(256, 128)
    copies[9].wait()
    mixed[:, 256:384] = spectra.astype(BF16)
    for step, low, high in ((1, 1, 3), (2, 0, 4)):
        straight = phase_v[2 * step - 2] * spectra
        crossed = phase_v[2 * step - 1] * swapped
        mixed[:, 128 * high : 128 * high + 128] = (straight + crossed).astype(BF16)
        mixed[:, 128 * low : 128 * low + 128] = (straight - crossed).astype(BF16)

    copies[8].wait()
    sums = nt(mixed[...], t2[...]).reshape(BANDS, 8, 256)
    near = swap_blocks(sums[:, :, 0:128])
    far = swap_blocks(sums[:, :, 128:256])
    packed[...] = jnp.concatenate([near, far], axis=1).astype(BF16)

    pl.semaphore_wait(rows_in, 3)

    def send(p):
        pltpu.make_async_remote_copy(
            src_ref=packed.at[p], dst_ref=received.at[me],
            send_sem=a2a_send, recv_sem=a2a_recv,
            device_id={"lat": p}, device_id_type=pl.DeviceIdType.MESH,
        ).start()

    pl.when(me != 1)(functools.partial(send, 1))
    for p in others:
        pl.when(p != 1)(functools.partial(send, p))
    received[me] = packed[me]
    copies[10].wait()
    some = pltpu.make_async_remote_copy(
        src_ref=packed.at[pl.ds(0, BANDS - 1)], dst_ref=received.at[pl.ds(0, BANDS - 1)],
        send_sem=a2a_send, recv_sem=a2a_recv,
        device_id={"lat": lax.rem(me + 1, BANDS)}, device_id_type=pl.DeviceIdType.MESH,
    )
    some.wait_recv()

    parts = received[...].astype(F32)
    near = parts[:, 0:8, :]
    far = parts[:, 8:16, :]
    none = jnp.zeros((1, 8, 128), F32)
    above = jnp.concatenate([none, far[:-1]], axis=0)
    below = jnp.concatenate([far[1:], none], axis=0)
    first = lax.broadcasted_iota(jnp.int32, near.shape, 1) < 4
    rows = (near + jnp.where(first, above, below)).reshape(LAT, 128)
    lines = rows.T.astype(BF16)
    for m in range(OWN):
        left = jnp.concatenate([lines[16 * m : 16 * m + 16], lines[64 + 16 * m : 80 + 16 * m]], axis=0)
        done = jnp.dot(left, table_v[m], preferred_element_type=F32)
        for q in range(2):
            for a in range(2):
                result[m, q, pl.ds(a, CH, stride=2), :] = done[
                    16 * a : 16 * a + 16, 128 * q : 128 * q + 128
                ]
    some.wait_send()


def store(source, target, semaphore):
    copy = pltpu.make_async_copy(source, target, semaphore)
    copy.start()
    copy.wait()


@functools.cache
def constants():
    return (
        edge_rows(), spread_first(), spread_second(), placed_rows(), fourier_rows(),
        phase_rows(), projection_table(),
    )


def per_device(atmosphere, first_weight, first_bias, second_weight):
    edge, spread1, spread2, placed, fourier, phase, table = constants()
    operands = (
        atmosphere.reshape(CH * ROWS, LON),
        first_weight.transpose(2, 3, 0, 1),
        first_bias.reshape(1, CH),
        second_weight.transpose(2, 3, 0, 1),
        edge, spread1, spread2, placed, fourier, phase, table,
    )
    scratch = [
        pltpu.VMEM((640, LON), BF16),
        pltpu.VMEM((320, LON), BF16),
        pltpu.VMEM((5, 5, CH, CH), BF16),
        pltpu.VMEM((1, CH), F32),
        pltpu.VMEM((5, 5, CH, CH), BF16),
        pltpu.VMEM(edge.shape, BF16),
        pltpu.VMEM(spread1.shape, BF16),
        pltpu.VMEM(spread2.shape, BF16),
        pltpu.VMEM(fourier.shape, BF16),
        pltpu.VMEM(phase.shape, F32),
        pltpu.VMEM(table.shape[1:], BF16),
        pltpu.VMEM((128, 640), BF16),
        pltpu.VMEM((64, 320), BF16),
        pltpu.VMEM((256, 768), BF16),
        pltpu.VMEM((64, LON), BF16),
        pltpu.VMEM((128, LON), F32),
        pltpu.VMEM((128, LON), BF16),
        pltpu.VMEM((256, 768), BF16),
        pltpu.VMEM((BANDS, 16, 128), BF16),
        pltpu.VMEM((BANDS, 16, 128), BF16),
        pltpu.SemaphoreType.DMA((11,)),
        pltpu.SemaphoreType.DMA((2,)),
        pltpu.SemaphoreType.DMA((2,)),
        pltpu.SemaphoreType.DMA,
        pltpu.SemaphoreType.DMA,
        pltpu.SemaphoreType.REGULAR,
    ]
    spectrum = pl.pallas_call(
        kernel,
        out_shape=pltpu.VMEM((OWN, 2, 2 * CH, 128), F32),
        in_specs=[pl.BlockSpec(memory_space=pltpu.HBM)] * len(operands),
        out_specs=pl.BlockSpec(memory_space=pltpu.VMEM),
        scratch_shapes=scratch,
        compiler_params=pltpu.CompilerParams(
            collective_id=0, has_side_effects=True, vmem_limit_bytes=56 * 1024 * 1024
        ),
        name="encoder",
    )(*operands)
    spectrum = pl.pallas_call(
        store,
        out_shape=jax.ShapeDtypeStruct((OWN, 2, 2 * CH, 128), F32),
        in_specs=[pl.BlockSpec(memory_space=pl.ANY)],
        compiler_params=pltpu.CompilerParams(vmem_limit_bytes=1024 * 1024),
        out_specs=pl.BlockSpec(memory_space=pltpu.HBM),
        scratch_shapes=[pltpu.SemaphoreType.DMA],
        name="store",
    )(spectrum)
    return spectrum.reshape(OWN, 2, CH, 2, 128)


def solution(mesh):
    placed = (
        P("chan", "lat", None),
        P("chan", None, None, None),
        P("chan"),
        P("chan", None, None, None),
    )
    return jax.shard_map(
        per_device,
        mesh=mesh,
        in_specs=placed,
        out_specs=P("lat", None, "chan", None, None),
        check_vma=False,
    )
```

```python
import functools
import math

import jax
import jax.numpy as jnp
import numpy as np
from jax import lax
from jax.experimental import pallas as pl
from jax.experimental.pallas import tpu as pltpu
from jax.sharding import PartitionSpec as P

ORDERS = 128
DEGREES = 256
LAT = 256
LON = 1536
BANDS = 32
ROWS = 8
CH = 16
OWN = ORDERS // BANDS
BF16 = jnp.bfloat16
F32 = jnp.float32


def fourier_rows():
    orders = np.arange(1, ORDERS + 1)
    places = np.arange(LON)
    phases = (orders[:, None] * places[None, :] % LON) * (2.0 * math.pi / LON)
    real = np.cos(phases) / math.sqrt(LON)
    imag = -np.sin(phases) / math.sqrt(LON)
    both = np.stack([real.reshape(BANDS, OWN, LON), imag.reshape(BANDS, OWN, LON)], axis=1)
    return both.reshape(2 * ORDERS, LON).T.astype(BF16)


def phase_rows():
    orders = np.arange(1, ORDERS + 1).reshape(BANDS, OWN)
    out = []
    for step in (1, 2):
        angle = 2.0 * math.pi * step * orders / LON
        cosine = np.stack([np.cos(angle), np.cos(angle)], axis=1).reshape(2 * ORDERS)
        sine = np.stack([-np.sin(angle), np.sin(angle)], axis=1).reshape(2 * ORDERS)
        out += [cosine, sine]
    table = np.stack(out)[:, :, None]
    return np.broadcast_to(table, (4, 2 * ORDERS, 128)).astype(np.float32).copy()


def projection_table():
    half = LAT // 2
    single = np.float32
    theta = (math.pi * (np.arange(half) + 0.5) / LAT).astype(single)
    cosine, sine = np.cos(theta)[None, :], np.sin(theta)[None, :]
    order = np.arange(1, ORDERS + 1, dtype=single)[:, None]
    gamma = np.vectorize(math.lgamma, otypes=[single])
    log_diag = (
        single(0.5)
        * (
            np.log((2 * order + 1) / 2)
            + gamma(2 * order + 1)
            - order * single(math.log(4.0))
            - 2 * gamma(order + 1)
        )
        + order * np.log(sine)
    )

    def normal(value):
        return np.where(np.abs(value) < np.finfo(single).tiny, single(0.0), value)

    diagonal = normal(np.exp(log_diag))
    latest = np.zeros_like(diagonal)
    before = np.zeros_like(diagonal)
    stacked = np.zeros((DEGREES, ORDERS, half), single)
    for degree in range(DEGREES):
        real = single(degree)
        spread = np.maximum(real * real - order * order, single(1.0))
        raising = np.sqrt(np.maximum(4 * real * real - 1, single(1.0)) / spread)
        previous = real - 1
        lowering = np.sqrt(
            np.maximum(previous * previous - order * order, single(0.0))
            / np.maximum(4 * previous * previous - 1, single(1.0))
        )
        raised = normal(
            raising * normal(normal(cosine * latest) - normal(lowering * before))
        )
        result = np.where(order == real, diagonal, np.where(order < real, raised, single(0.0)))
        stacked[degree] = result
        latest, before = result, latest
    weighted = stacked * (single(math.pi) * sine / single(math.sqrt(LAT)))[None]
    weighted = weighted.astype(BF16).astype(single)
    degrees = np.arange(DEGREES)[:, None, None]
    numbers = np.arange(1, ORDERS + 1)[None, :, None]
    sign = np.where((degrees + numbers) % 2 == 0, 1.0, -1.0).astype(np.float32)
    whole = np.concatenate([weighted, (weighted * sign)[:, :, ::-1]], axis=2)
    whole = whole.reshape(DEGREES // 2, 2, ORDERS, LAT).transpose(2, 3, 1, 0)
    return whole.reshape(BANDS, OWN, LAT, DEGREES).astype(BF16)


EDGE = (0, 1, 6, 7)
SLOTS = (0, 1, 2, 3, 4, 5, 6, 7, 8, 9, -2, -1)


def spread_first():
    own = np.zeros((128, ROWS, CH, ROWS), np.float32)
    halo = np.zeros((128, 4, 2, CH, 2), np.float32)
    for dy in range(5):
        for i in range(CH):
            for y in range(ROWS):
                row = y + dy - 2
                if 0 <= row < ROWS:
                    own[dy * CH + i, y, i, row] = 1.0
                elif row < 0:
                    halo[dy * CH + i, EDGE.index(y), 0, i, row + 2] = 1.0
                else:
                    halo[dy * CH + i, EDGE.index(y), 1, i, row - ROWS] = 1.0
    return np.concatenate([own.reshape(128, -1), halo.reshape(128, -1)], axis=1).astype(BF16)


def spread_second():
    out = np.zeros((128, len(SLOTS), ROWS, CH), np.float32)
    for dy in range(5):
        for i in range(CH):
            for at, slot in enumerate(SLOTS):
                row = slot + dy - 2
                if 0 <= row < ROWS:
                    out[dy * CH + i, at, row, i] = 1.0
    return out.reshape(128, -1).astype(BF16)


def edge_rows():
    out = np.zeros((2, CH, 2, CH, ROWS), np.float32)
    for c in range(CH):
        for t in range(2):
            out[0, c, t, c, t] = 1.0
            out[1, c, t, c, ROWS - 2 + t] = 1.0
    return out.reshape(64, 128).astype(BF16)


def placed_rows():
    out = np.zeros((16, CH, CH, ROWS), np.float32)
    for c in range(CH):
        for y in range(ROWS):
            out[y, c, c, y] = 1.0
    return out.reshape(256, 128).astype(BF16)


def nt(a, b):
    return lax.dot_general(a, b, (((1,), (1,)), ((), ())), preferred_element_type=F32)


def gelu(x):
    return 0.5 * x * (1.0 + lax.erf(x * math.sqrt(0.5)))


def swap_blocks(x):
    sub = lax.broadcasted_iota(jnp.int32, x.shape, 1)
    block = lax.broadcasted_iota(jnp.int32, x.shape, 2) // CH
    for bit in (1, 2, 4):
        high_sub = (sub & bit) != 0
        high_block = (block & bit) != 0
        lane = CH * bit
        down = pltpu.roll(pltpu.roll(x, 8 - bit, 1), lane, 2)
        up = pltpu.roll(pltpu.roll(x, bit, 1), 128 - lane, 2)
        x = jnp.where(high_sub == high_block, x, jnp.where(high_sub, up, down))
    return x


def base_of(weight):
    pieces = [weight[dy].reshape(5 * CH, CH).astype(F32) for dy in range(5)]
    pieces.append(jnp.zeros((5 * CH, 128 - 5 * CH), F32))
    return jnp.concatenate(pieces, axis=1).astype(BF16)


def peers(me):
    z, x, core = me // 8, (me // 2) % 4, me % 2
    depths = [(3, 3 - z), (2, (z + 2) % 4), (1, (z // 2) * 2 + 1 - z % 2), (0, z)]
    widths = [(2, (x + 2) % 4), (1, (x + 1) % 4), (1, (x + 3) % 4), (0, x)]
    pairs = sorted(
        ((far + wide, far, n, depth, width)
         for far, depth in depths
         for n, (wide, width) in enumerate(widths)),
        key=lambda pair: (-pair[0], -pair[1], pair[2]),
    )
    found = []
    for total, _, _, depth, width in pairs:
        for twin in (1 - core, core):
            if total > 0 or twin is not core:
                found.append((depth * 4 + width) * 2 + twin)
    return found


def kernel(
    atm, w1, bias, w2, edge, spread1, spread2, placed, fourier, phase, table, result,
    shifted, halo, w1_v, bias_v, w2_v, edge_v, spread1_v, spread2_v, fourier_v, phase_v, table_v,
    t1, t1h, t2, t2n, hsend, acc, hidden, mixed, packed, received,
    load_sem, halo_send, halo_recv, a2a_send, a2a_recv, rows_in,
):
    me = lax.axis_index("lat")
    barrier = pltpu.get_barrier_semaphore()

    loads = [
        (atm, shifted.at[pl.ds(256, 128), :]),
        (edge, edge_v),
        (w1, w1_v),
        (spread1, spread1_v),
        (bias, bias_v),
        (w2, w2_v),
        (spread2, spread2_v),
        (fourier, fourier_v),
        (placed, t2.at[:, pl.ds(640, 128)]),
        (phase, phase_v),
        (table.at[me], table_v),
    ]
    copies = [
        pltpu.make_async_copy(source, target, load_sem.at[n])
        for n, (source, target) in enumerate(loads)
    ]
    column, depth = me % 8, me // 8
    line = [8 * ((depth + k) % 4) + column for k in (1, 2, 3)]
    row = [8 * depth + (column + k) % 8 for k in (1, 7, 2, 6, 3, 5, 4)]

    def tell(semaphore, other):
        pl.semaphore_signal(
            semaphore, inc=1, device_id={"lat": other}, device_id_type=pl.DeviceIdType.MESH
        )

    step = jnp.where(column == 7, 1, -1)
    crossing = ((column == 7) & (me < BANDS - 1)) | ((column == 0) & (me > 0))

    for other in row[:2]:
        tell(barrier, other)

    @pl.when(crossing)
    def _():
        tell(barrier, me + step)

    copies[0].start()
    copies[1].start()
    for other in row[2:] + line:
        tell(barrier, other)

    for copy in copies[2:]:
        copy.start()

    copies[0].wait()
    copies[1].wait()
    hsend[...] = jnp.dot(
        edge_v[...], shifted[256:384, :], preferred_element_type=F32
    ).astype(BF16)

    pl.semaphore_wait(barrier, jnp.where(crossing, 11, 10))

    up = lax.max(me - 1, 0)
    down = lax.min(me + 1, BANDS - 1)
    to_up = pltpu.make_async_remote_copy(
        src_ref=hsend.at[pl.ds(0, 32), :], dst_ref=halo.at[pl.ds(160, 32), :],
        send_sem=halo_send.at[0], recv_sem=halo_recv.at[0],
        device_id={"lat": up}, device_id_type=pl.DeviceIdType.MESH,
    )
    to_down = pltpu.make_async_remote_copy(
        src_ref=hsend.at[pl.ds(32, 32), :], dst_ref=halo.at[pl.ds(128, 32), :],
        send_sem=halo_send.at[1], recv_sem=halo_recv.at[1],
        device_id={"lat": down}, device_id_type=pl.DeviceIdType.MESH,
    )

    @pl.when(me > 0)
    def _():
        to_up.start()

    @pl.when(me < BANDS - 1)
    def _():
        to_down.start()

    for other in line:
        tell(rows_in, other)

    copies[2].wait()
    copies[3].wait()
    res1 = jnp.dot(base_of(w1_v), spread1_v[...], preferred_element_type=F32).astype(BF16)
    for dx in range(5):
        for y in range(ROWS):
            t1[16 * y : 16 * y + 16, 128 * dx : 128 * dx + 128] = res1[
                16 * dx : 16 * dx + 16, 128 * y : 128 * y + 128
            ]
        for e in range(4):
            t1h[16 * e : 16 * e + 16, 64 * dx : 64 * dx + 64] = res1[
                16 * dx : 16 * dx + 16, 1024 + 64 * e : 1088 + 64 * e
            ]

    own = shifted[256:384, :].astype(F32)
    for dx in (0, 1, 3, 4):
        shifted[128 * dx : 128 * dx + 128, :] = pltpu.roll(own, (2 - dx) % LON, 1).astype(BF16)
    copies[4].wait()
    eye = lax.broadcasted_iota(jnp.int32, (CH, CH), 0) == lax.broadcasted_iota(
        jnp.int32, (CH, CH), 1
    )
    column = jnp.sum(
        jnp.where(eye, jnp.broadcast_to(bias_v[...], (CH, CH)), 0.0), axis=1, keepdims=True
    )
    offsets = jnp.concatenate([column] * ROWS, axis=0)
    acc[...] = jnp.dot(t1[...], shifted[...], preferred_element_type=F32) + offsets
    hidden[32:96, :] = gelu(acc[32:96, :]).astype(BF16)

    copies[5].wait()
    copies[6].wait()
    res2 = jnp.dot(base_of(w2_v), spread2_v[...], preferred_element_type=F32).astype(BF16)
    for at, slot in enumerate(SLOTS):
        row = 16 * (slot % 16)
        for dx in range(5):
            t2[row : row + 16, 128 * dx : 128 * dx + 128] = res2[
                16 * dx : 16 * dx + 16, 128 * at : 128 * at + 128
            ]
    t2[160:224, 0:640] = jnp.zeros((64, 640), BF16)
    copies[7].wait()
    mixed[:, 640:768] = jnp.dot(
        shifted[256:384, :], fourier_v[...], preferred_element_type=F32
    ).T.astype(BF16)

    copies[8].wait()
    t2n[...] = t2[...].astype(F32).T.astype(BF16)

    @pl.when(me > 0)
    def _():
        to_up.wait_send()
        to_down.wait_recv()

    @pl.when(me < BANDS - 1)
    def _():
        to_down.wait_send()
        to_up.wait_recv()

    @pl.when(me == 0)
    def _():
        halo[128:160, :] = jnp.zeros((32, LON), BF16)

    @pl.when(me == BANDS - 1)
    def _():
        halo[160:192, :] = jnp.zeros((32, LON), BF16)

    rim = halo[128:192, :].astype(F32)
    for dx in (0, 1, 3, 4):
        halo[64 * dx : 64 * dx + 64, :] = pltpu.roll(rim, (2 - dx) % LON, 1).astype(BF16)
    more = jnp.dot(t1h[...], halo[...], preferred_element_type=F32)
    hidden[0:32, :] = gelu(acc[0:32, :] + more[0:32]).astype(BF16)
    hidden[96:128, :] = gelu(acc[96:128, :] + more[32:64]).astype(BF16)

    spectra = jnp.dot(hidden[...], fourier_v[...], preferred_element_type=F32).T
    swapped = pltpu.roll(spectra.reshape(BANDS, 8, 128), 4, 1).reshape(256, 128)
    copies[9].wait()
    mixed[:, 256:384] = spectra.astype(BF16)
    for step, low, high in ((1, 1, 3), (2, 0, 4)):
        straight = phase_v[2 * step - 2] * spectra
        crossed = phase_v[2 * step - 1] * swapped
        mixed[:, 128 * high : 128 * high + 128] = (straight + crossed).astype(BF16)
        mixed[:, 128 * low : 128 * low + 128] = (straight - crossed).astype(BF16)

    sums = jnp.dot(mixed[...], t2n[...], preferred_element_type=F32).reshape(BANDS, 8, 256)
    near = swap_blocks(sums[:, :, 0:128])
    far = swap_blocks(sums[:, :, 128:256])
    packed[...] = jnp.concatenate([near, far], axis=1).astype(BF16)

    pl.semaphore_wait(rows_in, 3)

    others = peers(me)

    def send(p):
        pltpu.make_async_remote_copy(
            src_ref=packed.at[p], dst_ref=received.at[me],
            send_sem=a2a_send, recv_sem=a2a_recv,
            device_id={"lat": p}, device_id_type=pl.DeviceIdType.MESH,
        ).start()

    pl.when(me != 1)(functools.partial(send, 1))
    for p in others:
        pl.when(p != 1)(functools.partial(send, p))
    received[me] = packed[me]
    copies[10].wait()
    some = pltpu.make_async_remote_copy(
        src_ref=packed.at[pl.ds(0, BANDS - 1)], dst_ref=received.at[pl.ds(0, BANDS - 1)],
        send_sem=a2a_send, recv_sem=a2a_recv,
        device_id={"lat": lax.rem(me + 1, BANDS)}, device_id_type=pl.DeviceIdType.MESH,
    )
    some.wait_recv()

    parts = received[...].astype(F32)
    near = parts[:, 0:8, :]
    far = parts[:, 8:16, :]
    none = jnp.zeros((1, 8, 128), F32)
    above = jnp.concatenate([none, far[:-1]], axis=0)
    below = jnp.concatenate([far[1:], none], axis=0)
    first = lax.broadcasted_iota(jnp.int32, near.shape, 1) < 4
    rows = (near + jnp.where(first, above, below)).reshape(LAT, 128)
    lines = rows.T.astype(BF16)
    for m in range(OWN):
        left = jnp.concatenate([lines[16 * m : 16 * m + 16], lines[64 + 16 * m : 80 + 16 * m]], axis=0)
        done = jnp.dot(left, table_v[m], preferred_element_type=F32)
        for q in range(2):
            for a in range(2):
                result[m, q, pl.ds(a, CH, stride=2), :] = done[
                    16 * a : 16 * a + 16, 128 * q : 128 * q + 128
                ]
    some.wait_send()


def store(source, target, semaphore):
    copy = pltpu.make_async_copy(source, target, semaphore)
    copy.start()
    copy.wait()


@functools.cache
def constants():
    return (
        edge_rows(), spread_first(), spread_second(), placed_rows(), fourier_rows(),
        phase_rows(), projection_table(),
    )


def per_device(atmosphere, first_weight, first_bias, second_weight):
    edge, spread1, spread2, placed, fourier, phase, table = constants()
    operands = (
        atmosphere.reshape(CH * ROWS, LON),
        first_weight.transpose(2, 3, 0, 1),
        first_bias.reshape(1, CH),
        second_weight.transpose(2, 3, 0, 1),
        edge, spread1, spread2, placed, fourier, phase, table,
    )
    scratch = [
        pltpu.VMEM((640, LON), BF16),
        pltpu.VMEM((320, LON), BF16),
        pltpu.VMEM((5, 5, CH, CH), BF16),
        pltpu.VMEM((1, CH), F32),
        pltpu.VMEM((5, 5, CH, CH), BF16),
        pltpu.VMEM(edge.shape, BF16),
        pltpu.VMEM(spread1.shape, BF16),
        pltpu.VMEM(spread2.shape, BF16),
        pltpu.VMEM(fourier.shape, BF16),
        pltpu.VMEM(phase.shape, F32),
        pltpu.VMEM(table.shape[1:], BF16),
        pltpu.VMEM((128, 640), BF16),
        pltpu.VMEM((64, 320), BF16),
        pltpu.VMEM((256, 768), BF16),
        pltpu.VMEM((768, 256), BF16),
        pltpu.VMEM((64, LON), BF16),
        pltpu.VMEM((128, LON), F32),
        pltpu.VMEM((128, LON), BF16),
        pltpu.VMEM((256, 768), BF16),
        pltpu.VMEM((BANDS, 16, 128), BF16),
        pltpu.VMEM((BANDS, 16, 128), BF16),
        pltpu.SemaphoreType.DMA((11,)),
        pltpu.SemaphoreType.DMA((2,)),
        pltpu.SemaphoreType.DMA((2,)),
        pltpu.SemaphoreType.DMA,
        pltpu.SemaphoreType.DMA,
        pltpu.SemaphoreType.REGULAR,
    ]
    spectrum = pl.pallas_call(
        kernel,
        out_shape=pltpu.VMEM((OWN, 2, 2 * CH, 128), F32),
        in_specs=[pl.BlockSpec(memory_space=pltpu.HBM)] * len(operands),
        out_specs=pl.BlockSpec(memory_space=pltpu.VMEM),
        scratch_shapes=scratch,
        compiler_params=pltpu.CompilerParams(
            collective_id=0, has_side_effects=True, vmem_limit_bytes=56 * 1024 * 1024
        ),
        name="encoder",
    )(*operands)
    spectrum = pl.pallas_call(
        store,
        out_shape=jax.ShapeDtypeStruct((OWN, 2, 2 * CH, 128), F32),
        in_specs=[pl.BlockSpec(memory_space=pl.ANY)],
        compiler_params=pltpu.CompilerParams(vmem_limit_bytes=1024 * 1024),
        out_specs=pl.BlockSpec(memory_space=pltpu.HBM),
        scratch_shapes=[pltpu.SemaphoreType.DMA],
        name="store",
    )(spectrum)
    return spectrum.reshape(OWN, 2, CH, 2, 128)


def solution(mesh):
    placed = (
        P("chan", "lat", None),
        P("chan", None, None, None),
        P("chan"),
        P("chan", None, None, None),
    )
    return jax.shard_map(
        per_device,
        mesh=mesh,
        in_specs=placed,
        out_specs=P("lat", None, "chan", None, None),
        check_vma=False,
    )
```

```python
import functools
import math

import jax
import jax.numpy as jnp
import numpy as np
from jax import lax
from jax.experimental import pallas as pl
from jax.experimental.pallas import tpu as pltpu
from jax.sharding import PartitionSpec as P

ORDERS = 128
DEGREES = 256
LAT = 256
LON = 1536
BANDS = 32
ROWS = 8
CH = 16
OWN = ORDERS // BANDS
BF16 = jnp.bfloat16
F32 = jnp.float32


def fourier_rows():
    orders = np.arange(1, ORDERS + 1)
    places = np.arange(LON)
    phases = (orders[:, None] * places[None, :] % LON) * (2.0 * math.pi / LON)
    real = np.cos(phases) / math.sqrt(LON)
    imag = -np.sin(phases) / math.sqrt(LON)
    both = np.stack([real.reshape(BANDS, OWN, LON), imag.reshape(BANDS, OWN, LON)], axis=1)
    return both.reshape(2 * ORDERS, LON).T.astype(BF16)


def phase_rows():
    orders = np.arange(1, ORDERS + 1).reshape(BANDS, OWN)
    out = []
    for step in (1, 2):
        angle = 2.0 * math.pi * step * orders / LON
        cosine = np.stack([np.cos(angle), np.cos(angle)], axis=1).reshape(2 * ORDERS)
        sine = np.stack([-np.sin(angle), np.sin(angle)], axis=1).reshape(2 * ORDERS)
        out += [cosine, sine]
    table = np.stack(out)[:, :, None]
    return np.broadcast_to(table, (4, 2 * ORDERS, 128)).astype(np.float32).copy()


def projection_table():
    half = LAT // 2
    single = np.float32
    theta = (math.pi * (np.arange(half) + 0.5) / LAT).astype(single)
    cosine, sine = np.cos(theta)[None, :], np.sin(theta)[None, :]
    order = np.arange(1, ORDERS + 1, dtype=single)[:, None]
    gamma = np.vectorize(math.lgamma, otypes=[single])
    log_diag = (
        single(0.5)
        * (
            np.log((2 * order + 1) / 2)
            + gamma(2 * order + 1)
            - order * single(math.log(4.0))
            - 2 * gamma(order + 1)
        )
        + order * np.log(sine)
    )

    def normal(value):
        return np.where(np.abs(value) < np.finfo(single).tiny, single(0.0), value)

    diagonal = normal(np.exp(log_diag))
    latest = np.zeros_like(diagonal)
    before = np.zeros_like(diagonal)
    stacked = np.zeros((DEGREES, ORDERS, half), single)
    for degree in range(DEGREES):
        real = single(degree)
        spread = np.maximum(real * real - order * order, single(1.0))
        raising = np.sqrt(np.maximum(4 * real * real - 1, single(1.0)) / spread)
        previous = real - 1
        lowering = np.sqrt(
            np.maximum(previous * previous - order * order, single(0.0))
            / np.maximum(4 * previous * previous - 1, single(1.0))
        )
        raised = normal(
            raising * normal(normal(cosine * latest) - normal(lowering * before))
        )
        result = np.where(order == real, diagonal, np.where(order < real, raised, single(0.0)))
        stacked[degree] = result
        latest, before = result, latest
    weighted = stacked * (single(math.pi) * sine / single(math.sqrt(LAT)))[None]
    weighted = weighted.astype(BF16).astype(single)
    degrees = np.arange(DEGREES)[:, None, None]
    numbers = np.arange(1, ORDERS + 1)[None, :, None]
    sign = np.where((degrees + numbers) % 2 == 0, 1.0, -1.0).astype(np.float32)
    whole = np.concatenate([weighted, (weighted * sign)[:, :, ::-1]], axis=2)
    whole = whole.reshape(DEGREES // 2, 2, ORDERS, LAT).transpose(2, 3, 1, 0)
    return whole.reshape(BANDS, OWN, LAT, DEGREES).astype(BF16)


EDGE = (0, 1, 6, 7)
SLOTS = (0, 1, 2, 3, 4, 5, 6, 7, 8, 9, -2, -1)


def spread_first():
    own = np.zeros((128, ROWS, CH, ROWS), np.float32)
    halo = np.zeros((128, 4, 2, CH, 2), np.float32)
    for dy in range(5):
        for i in range(CH):
            for y in range(ROWS):
                row = y + dy - 2
                if 0 <= row < ROWS:
                    own[dy * CH + i, y, i, row] = 1.0
                elif row < 0:
                    halo[dy * CH + i, EDGE.index(y), 0, i, row + 2] = 1.0
                else:
                    halo[dy * CH + i, EDGE.index(y), 1, i, row - ROWS] = 1.0
    return np.concatenate([own.reshape(128, -1), halo.reshape(128, -1)], axis=1).astype(BF16)


def spread_second():
    out = np.zeros((128, len(SLOTS), ROWS, CH), np.float32)
    for dy in range(5):
        for i in range(CH):
            for at, slot in enumerate(SLOTS):
                row = slot + dy - 2
                if 0 <= row < ROWS:
                    out[dy * CH + i, at, row, i] = 1.0
    return out.reshape(128, -1).astype(BF16)


def edge_rows():
    out = np.zeros((2, CH, 2, CH, ROWS), np.float32)
    for c in range(CH):
        for t in range(2):
            out[0, c, t, c, t] = 1.0
            out[1, c, t, c, ROWS - 2 + t] = 1.0
    return out.reshape(64, 128).astype(BF16)


def placed_rows():
    out = np.zeros((16, CH, CH, ROWS), np.float32)
    for c in range(CH):
        for y in range(ROWS):
            out[y, c, c, y] = 1.0
    return out.reshape(256, 128).astype(BF16)


def nt(a, b):
    return lax.dot_general(a, b, (((1,), (1,)), ((), ())), preferred_element_type=F32)


def gelu(x):
    return 0.5 * x * (1.0 + lax.erf(x * math.sqrt(0.5)))


def swap_blocks(x):
    sub = lax.broadcasted_iota(jnp.int32, x.shape, 1)
    block = lax.broadcasted_iota(jnp.int32, x.shape, 2) // CH
    for bit in (1, 2, 4):
        high_sub = (sub & bit) != 0
        high_block = (block & bit) != 0
        lane = CH * bit
        down = pltpu.roll(pltpu.roll(x, 8 - bit, 1), lane, 2)
        up = pltpu.roll(pltpu.roll(x, bit, 1), 128 - lane, 2)
        x = jnp.where(high_sub == high_block, x, jnp.where(high_sub, up, down))
    return x


def base_of(weight):
    pieces = [weight[dy].reshape(5 * CH, CH).astype(F32) for dy in range(5)]
    pieces.append(jnp.zeros((5 * CH, 128 - 5 * CH), F32))
    return jnp.concatenate(pieces, axis=1).astype(BF16)


def peers(me):
    z, x, core = me // 8, (me // 2) % 4, me % 2
    depths = [(3, 3 - z), (2, (z + 2) % 4), (1, (z // 2) * 2 + 1 - z % 2), (0, z)]
    widths = [(2, (x + 2) % 4), (1, (x + 1) % 4), (1, (x + 3) % 4), (0, x)]
    pairs = sorted(
        ((far + wide, far, n, depth, width)
         for far, depth in depths
         for n, (wide, width) in enumerate(widths)),
        key=lambda pair: (-pair[0], -pair[1], pair[2]),
    )
    found = []
    for total, _, _, depth, width in pairs:
        for twin in (1 - core, core):
            if total > 0 or twin is not core:
                found.append((depth * 4 + width) * 2 + twin)
    return found


def kernel(
    atm, w1, bias, w2, edge, spread1, spread2, placed, fourier, phase, table, result,
    shifted, halo, w1_v, bias_v, w2_v, edge_v, spread1_v, spread2_v, fourier_v, phase_v, table_v,
    t1, t1h, t2, t2n, hsend, acc, hidden, mixed, packed, received,
    load_sem, halo_send, halo_recv, a2a_send, a2a_recv, rows_in,
):
    me = lax.axis_index("lat")
    barrier = pltpu.get_barrier_semaphore()

    loads = [
        (atm, shifted.at[pl.ds(256, 128), :]),
        (edge, edge_v),
        (w1, w1_v),
        (spread1, spread1_v),
        (bias, bias_v),
        (w2, w2_v),
        (spread2, spread2_v),
        (fourier, fourier_v),
        (placed, t2.at[:, pl.ds(640, 128)]),
        (phase, phase_v),
        (table.at[me], table_v),
    ]
    copies = [
        pltpu.make_async_copy(source, target, load_sem.at[n])
        for n, (source, target) in enumerate(loads)
    ]
    column, depth = me % 8, me // 8
    line = [8 * ((depth + k) % 4) + column for k in (1, 2, 3)]
    row = [8 * depth + (column + k) % 8 for k in (1, 7, 2, 6, 3, 5, 4)]

    def tell(semaphore, other):
        pl.semaphore_signal(
            semaphore, inc=1, device_id={"lat": other}, device_id_type=pl.DeviceIdType.MESH
        )

    step = jnp.where(column == 7, 1, -1)
    crossing = ((column == 7) & (me < BANDS - 1)) | ((column == 0) & (me > 0))

    for other in row[:2]:
        tell(barrier, other)

    @pl.when(crossing)
    def _():
        tell(barrier, me + step)

    copies[0].start()
    copies[1].start()
    for other in row[2:] + line:
        tell(barrier, other)

    for copy in copies[2:]:
        copy.start()

    copies[0].wait()
    copies[1].wait()
    hsend[...] = jnp.dot(
        edge_v[...], shifted[256:384, :], preferred_element_type=F32
    ).astype(BF16)

    pl.semaphore_wait(barrier, jnp.where(crossing, 11, 10))

    up = lax.max(me - 1, 0)
    down = lax.min(me + 1, BANDS - 1)
    to_up = pltpu.make_async_remote_copy(
        src_ref=hsend.at[pl.ds(0, 32), :], dst_ref=halo.at[1, pl.ds(64, 32), :],
        send_sem=halo_send.at[0], recv_sem=halo_recv.at[0],
        device_id={"lat": up}, device_id_type=pl.DeviceIdType.MESH,
    )
    to_down = pltpu.make_async_remote_copy(
        src_ref=hsend.at[pl.ds(32, 32), :], dst_ref=halo.at[0, pl.ds(64, 32), :],
        send_sem=halo_send.at[1], recv_sem=halo_recv.at[1],
        device_id={"lat": down}, device_id_type=pl.DeviceIdType.MESH,
    )

    @pl.when(me > 0)
    def _():
        to_up.start()

    @pl.when(me < BANDS - 1)
    def _():
        to_down.start()

    for other in line:
        tell(rows_in, other)

    copies[2].wait()
    copies[3].wait()
    res1 = jnp.dot(base_of(w1_v), spread1_v[...], preferred_element_type=F32).astype(BF16)
    for dx in range(5):
        for y in range(ROWS):
            t1[16 * y : 16 * y + 16, 128 * dx : 128 * dx + 128] = res1[
                16 * dx : 16 * dx + 16, 128 * y : 128 * y + 128
            ]
        for e in range(4):
            side, at = e // 2, 16 * (e % 2)
            start = 1024 + 64 * e + 32 * side
            t1h[side, at : at + 16, 32 * dx : 32 * dx + 32] = res1[
                16 * dx : 16 * dx + 16, start : start + 32
            ]

    own = shifted[256:384, :].astype(F32)
    for dx in (0, 1, 3, 4):
        shifted[128 * dx : 128 * dx + 128, :] = pltpu.roll(own, (2 - dx) % LON, 1).astype(BF16)
    copies[4].wait()
    eye = lax.broadcasted_iota(jnp.int32, (CH, CH), 0) == lax.broadcasted_iota(
        jnp.int32, (CH, CH), 1
    )
    column = jnp.sum(
        jnp.where(eye, jnp.broadcast_to(bias_v[...], (CH, CH)), 0.0), axis=1, keepdims=True
    )
    offsets = jnp.concatenate([column] * ROWS, axis=0)
    acc[...] = jnp.dot(t1[...], shifted[...], preferred_element_type=F32) + offsets
    hidden[32:96, :] = gelu(acc[32:96, :]).astype(BF16)

    copies[5].wait()
    copies[6].wait()
    res2 = jnp.dot(base_of(w2_v), spread2_v[...], preferred_element_type=F32).astype(BF16)
    for at, slot in enumerate(SLOTS):
        row = 16 * (slot % 16)
        for dx in range(5):
            t2[row : row + 16, 128 * dx : 128 * dx + 128] = res2[
                16 * dx : 16 * dx + 16, 128 * at : 128 * at + 128
            ]
    t2[160:224, 0:640] = jnp.zeros((64, 640), BF16)
    copies[7].wait()
    mixed[:, 640:768] = jnp.dot(
        shifted[256:384, :], fourier_v[...], preferred_element_type=F32
    ).T.astype(BF16)

    copies[8].wait()
    t2n[...] = t2[...].astype(F32).T.astype(BF16)

    @pl.when(me == 0)
    def _():
        halo[0, 64:96, :] = jnp.zeros((32, LON), BF16)

    @pl.when(me == BANDS - 1)
    def _():
        halo[1, 64:96, :] = jnp.zeros((32, LON), BF16)

    def edge_of(side):
        rim = halo[side, 64:96, :].astype(F32)
        for dx in (0, 1, 3, 4):
            halo[side, 32 * dx : 32 * dx + 32, :] = pltpu.roll(rim, (2 - dx) % LON, 1).astype(BF16)
        more = jnp.dot(t1h[side], halo[side], preferred_element_type=F32)
        rows = pl.ds(pl.multiple_of(96 * side, 32), 32)
        hidden[rows, :] = gelu(acc[rows, :] + more).astype(BF16)

    core = me % 2
    pl.when(core == 0)(to_up.wait_recv)
    pl.when(core == 1)(to_down.wait_recv)
    edge_of(1 - core)
    pl.when((core == 0) & (me > 0))(to_down.wait_recv)
    pl.when((core == 1) & (me < BANDS - 1))(to_up.wait_recv)
    edge_of(core)

    spectra = jnp.dot(hidden[...], fourier_v[...], preferred_element_type=F32).T
    swapped = pltpu.roll(spectra.reshape(BANDS, 8, 128), 4, 1).reshape(256, 128)
    copies[9].wait()
    mixed[:, 256:384] = spectra.astype(BF16)
    for step, low, high in ((1, 1, 3), (2, 0, 4)):
        straight = phase_v[2 * step - 2] * spectra
        crossed = phase_v[2 * step - 1] * swapped
        mixed[:, 128 * high : 128 * high + 128] = (straight + crossed).astype(BF16)
        mixed[:, 128 * low : 128 * low + 128] = (straight - crossed).astype(BF16)

    sums = jnp.dot(mixed[...], t2n[...], preferred_element_type=F32).reshape(BANDS, 8, 256)
    near = swap_blocks(sums[:, :, 0:128])
    far = swap_blocks(sums[:, :, 128:256])
    packed[...] = jnp.concatenate([near, far], axis=1).astype(BF16)

    pl.semaphore_wait(rows_in, 3)

    others = peers(me)

    def send(p):
        pltpu.make_async_remote_copy(
            src_ref=packed.at[p], dst_ref=received.at[me],
            send_sem=a2a_send, recv_sem=a2a_recv,
            device_id={"lat": p}, device_id_type=pl.DeviceIdType.MESH,
        ).start()

    pl.when(me != 1)(functools.partial(send, 1))
    for p in others:
        pl.when(p != 1)(functools.partial(send, p))
    received[me] = packed[me]
    copies[10].wait()
    some = pltpu.make_async_remote_copy(
        src_ref=packed.at[pl.ds(0, BANDS - 1)], dst_ref=received.at[pl.ds(0, BANDS - 1)],
        send_sem=a2a_send, recv_sem=a2a_recv,
        device_id={"lat": lax.rem(me + 1, BANDS)}, device_id_type=pl.DeviceIdType.MESH,
    )
    some.wait_recv()

    parts = received[...].astype(F32)
    near = parts[:, 0:8, :]
    far = parts[:, 8:16, :]
    none = jnp.zeros((1, 8, 128), F32)
    above = jnp.concatenate([none, far[:-1]], axis=0)
    below = jnp.concatenate([far[1:], none], axis=0)
    first = lax.broadcasted_iota(jnp.int32, near.shape, 1) < 4
    rows = (near + jnp.where(first, above, below)).reshape(LAT, 128)
    lines = rows.T.astype(BF16)
    for m in range(OWN):
        left = jnp.concatenate([lines[16 * m : 16 * m + 16], lines[64 + 16 * m : 80 + 16 * m]], axis=0)
        done = jnp.dot(left, table_v[m], preferred_element_type=F32)
        for q in range(2):
            for a in range(2):
                result[m, q, pl.ds(a, CH, stride=2), :] = done[
                    16 * a : 16 * a + 16, 128 * q : 128 * q + 128
                ]
    some.wait_send()
    pl.when(me > 0)(to_up.wait_send)
    pl.when(me < BANDS - 1)(to_down.wait_send)


def store(source, target, semaphore):
    copy = pltpu.make_async_copy(source, target, semaphore)
    copy.start()
    copy.wait()


@functools.cache
def constants():
    return (
        edge_rows(), spread_first(), spread_second(), placed_rows(), fourier_rows(),
        phase_rows(), projection_table(),
    )


def per_device(atmosphere, first_weight, first_bias, second_weight):
    edge, spread1, spread2, placed, fourier, phase, table = constants()
    operands = (
        atmosphere.reshape(CH * ROWS, LON),
        first_weight.transpose(2, 3, 0, 1),
        first_bias.reshape(1, CH),
        second_weight.transpose(2, 3, 0, 1),
        edge, spread1, spread2, placed, fourier, phase, table,
    )
    scratch = [
        pltpu.VMEM((640, LON), BF16),
        pltpu.VMEM((2, 160, LON), BF16),
        pltpu.VMEM((5, 5, CH, CH), BF16),
        pltpu.VMEM((1, CH), F32),
        pltpu.VMEM((5, 5, CH, CH), BF16),
        pltpu.VMEM(edge.shape, BF16),
        pltpu.VMEM(spread1.shape, BF16),
        pltpu.VMEM(spread2.shape, BF16),
        pltpu.VMEM(fourier.shape, BF16),
        pltpu.VMEM(phase.shape, F32),
        pltpu.VMEM(table.shape[1:], BF16),
        pltpu.VMEM((128, 640), BF16),
        pltpu.VMEM((2, 32, 160), BF16),
        pltpu.VMEM((256, 768), BF16),
        pltpu.VMEM((768, 256), BF16),
        pltpu.VMEM((64, LON), BF16),
        pltpu.VMEM((128, LON), F32),
        pltpu.VMEM((128, LON), BF16),
        pltpu.VMEM((256, 768), BF16),
        pltpu.VMEM((BANDS, 16, 128), BF16),
        pltpu.VMEM((BANDS, 16, 128), BF16),
        pltpu.SemaphoreType.DMA((11,)),
        pltpu.SemaphoreType.DMA((2,)),
        pltpu.SemaphoreType.DMA((2,)),
        pltpu.SemaphoreType.DMA,
        pltpu.SemaphoreType.DMA,
        pltpu.SemaphoreType.REGULAR,
    ]
    spectrum = pl.pallas_call(
        kernel,
        out_shape=pltpu.VMEM((OWN, 2, 2 * CH, 128), F32),
        in_specs=[pl.BlockSpec(memory_space=pltpu.HBM)] * len(operands),
        out_specs=pl.BlockSpec(memory_space=pltpu.VMEM),
        scratch_shapes=scratch,
        compiler_params=pltpu.CompilerParams(
            collective_id=0, has_side_effects=True, vmem_limit_bytes=56 * 1024 * 1024
        ),
        name="encoder",
    )(*operands)
    spectrum = pl.pallas_call(
        store,
        out_shape=jax.ShapeDtypeStruct((OWN, 2, 2 * CH, 128), F32),
        in_specs=[pl.BlockSpec(memory_space=pl.ANY)],
        compiler_params=pltpu.CompilerParams(vmem_limit_bytes=1024 * 1024),
        out_specs=pl.BlockSpec(memory_space=pltpu.HBM),
        scratch_shapes=[pltpu.SemaphoreType.DMA],
        name="store",
    )(spectrum)
    return spectrum.reshape(OWN, 2, CH, 2, 128)


def solution(mesh):
    placed = (
        P("chan", "lat", None),
        P("chan", None, None, None),
        P("chan"),
        P("chan", None, None, None),
    )
    return jax.shard_map(
        per_device,
        mesh=mesh,
        in_specs=placed,
        out_specs=P("lat", None, "chan", None, None),
        check_vma=False,
    )
```

```python
import functools
import math

import jax
import jax.numpy as jnp
import numpy as np
from jax import lax
from jax.experimental import pallas as pl
from jax.experimental.pallas import tpu as pltpu
from jax.sharding import PartitionSpec as P

ORDERS = 128
DEGREES = 256
LAT = 256
LON = 1536
BANDS = 32
ROWS = 8
CH = 16
OWN = ORDERS // BANDS
BF16 = jnp.bfloat16
F32 = jnp.float32


def fourier_rows():
    orders = np.arange(1, ORDERS + 1)
    places = np.arange(LON)
    phases = (orders[:, None] * places[None, :] % LON) * (2.0 * math.pi / LON)
    real = np.cos(phases) / math.sqrt(LON)
    imag = -np.sin(phases) / math.sqrt(LON)
    both = np.stack([real.reshape(BANDS, OWN, LON), imag.reshape(BANDS, OWN, LON)], axis=1)
    return both.reshape(2 * ORDERS, LON).T.astype(BF16)


def phase_rows():
    orders = np.arange(1, ORDERS + 1).reshape(BANDS, OWN)
    out = []
    for step in (1, 2):
        angle = 2.0 * math.pi * step * orders / LON
        cosine = np.stack([np.cos(angle), np.cos(angle)], axis=1).reshape(2 * ORDERS)
        sine = np.stack([-np.sin(angle), np.sin(angle)], axis=1).reshape(2 * ORDERS)
        out += [cosine, sine]
    table = np.stack(out)[:, :, None]
    return np.broadcast_to(table, (4, 2 * ORDERS, 128)).astype(np.float32).copy()


def projection_table():
    half = LAT // 2
    single = np.float32
    theta = (math.pi * (np.arange(half) + 0.5) / LAT).astype(single)
    cosine, sine = np.cos(theta)[None, :], np.sin(theta)[None, :]
    order = np.arange(1, ORDERS + 1, dtype=single)[:, None]
    gamma = np.vectorize(math.lgamma, otypes=[single])
    log_diag = (
        single(0.5)
        * (
            np.log((2 * order + 1) / 2)
            + gamma(2 * order + 1)
            - order * single(math.log(4.0))
            - 2 * gamma(order + 1)
        )
        + order * np.log(sine)
    )

    def normal(value):
        return np.where(np.abs(value) < np.finfo(single).tiny, single(0.0), value)

    diagonal = normal(np.exp(log_diag))
    latest = np.zeros_like(diagonal)
    before = np.zeros_like(diagonal)
    stacked = np.zeros((DEGREES, ORDERS, half), single)
    for degree in range(DEGREES):
        real = single(degree)
        spread = np.maximum(real * real - order * order, single(1.0))
        raising = np.sqrt(np.maximum(4 * real * real - 1, single(1.0)) / spread)
        previous = real - 1
        lowering = np.sqrt(
            np.maximum(previous * previous - order * order, single(0.0))
            / np.maximum(4 * previous * previous - 1, single(1.0))
        )
        raised = normal(
            raising * normal(normal(cosine * latest) - normal(lowering * before))
        )
        result = np.where(order == real, diagonal, np.where(order < real, raised, single(0.0)))
        stacked[degree] = result
        latest, before = result, latest
    weighted = stacked * (single(math.pi) * sine / single(math.sqrt(LAT)))[None]
    weighted = weighted.astype(BF16).astype(single)
    degrees = np.arange(DEGREES)[:, None, None]
    numbers = np.arange(1, ORDERS + 1)[None, :, None]
    sign = np.where((degrees + numbers) % 2 == 0, 1.0, -1.0).astype(np.float32)
    whole = np.concatenate([weighted, (weighted * sign)[:, :, ::-1]], axis=2)
    whole = whole.reshape(DEGREES // 2, 2, ORDERS, LAT).transpose(2, 3, 1, 0)
    return whole.reshape(BANDS, OWN, LAT, DEGREES).astype(BF16)


EDGE = (0, 1, 6, 7)
SLOTS = (0, 1, 2, 3, 4, 5, 6, 7, 8, 9, -2, -1)


def spread_first():
    own = np.zeros((128, ROWS, CH, ROWS), np.float32)
    halo = np.zeros((128, 4, 2, CH, 2), np.float32)
    for dy in range(5):
        for i in range(CH):
            for y in range(ROWS):
                row = y + dy - 2
                if 0 <= row < ROWS:
                    own[dy * CH + i, y, i, row] = 1.0
                elif row < 0:
                    halo[dy * CH + i, EDGE.index(y), 0, i, row + 2] = 1.0
                else:
                    halo[dy * CH + i, EDGE.index(y), 1, i, row - ROWS] = 1.0
    return np.concatenate([own.reshape(128, -1), halo.reshape(128, -1)], axis=1).astype(BF16)


def spread_second():
    out = np.zeros((128, len(SLOTS), ROWS, CH), np.float32)
    for dy in range(5):
        for i in range(CH):
            for at, slot in enumerate(SLOTS):
                row = slot + dy - 2
                if 0 <= row < ROWS:
                    out[dy * CH + i, at, row, i] = 1.0
    return out.reshape(128, -1).astype(BF16)


def edge_rows():
    out = np.zeros((2, CH, 2, CH, ROWS), np.float32)
    for c in range(CH):
        for t in range(2):
            out[0, c, t, c, t] = 1.0
            out[1, c, t, c, ROWS - 2 + t] = 1.0
    return out.reshape(64, 128).astype(BF16)


def placed_rows():
    out = np.zeros((16, CH, CH, ROWS), np.float32)
    for c in range(CH):
        for y in range(ROWS):
            out[y, c, c, y] = 1.0
    return out.reshape(256, 128).astype(BF16)


def nt(a, b):
    return lax.dot_general(a, b, (((1,), (1,)), ((), ())), preferred_element_type=F32)


def gelu(x):
    return 0.5 * x * (1.0 + lax.erf(x * math.sqrt(0.5)))


def swap_blocks(x):
    sub = lax.broadcasted_iota(jnp.int32, x.shape, 1)
    block = lax.broadcasted_iota(jnp.int32, x.shape, 2) // CH
    for bit in (1, 2, 4):
        high_sub = (sub & bit) != 0
        high_block = (block & bit) != 0
        lane = CH * bit
        down = pltpu.roll(pltpu.roll(x, 8 - bit, 1), lane, 2)
        up = pltpu.roll(pltpu.roll(x, bit, 1), 128 - lane, 2)
        x = jnp.where(high_sub == high_block, x, jnp.where(high_sub, up, down))
    return x


def base_of(weight):
    pieces = [weight[dy].reshape(5 * CH, CH).astype(F32) for dy in range(5)]
    pieces.append(jnp.zeros((5 * CH, 128 - 5 * CH), F32))
    return jnp.concatenate(pieces, axis=1).astype(BF16)


def peers(me):
    z, x, core = me // 8, (me // 2) % 4, me % 2
    depths = [(3, 3 - z), (2, (z + 2) % 4), (1, (z // 2) * 2 + 1 - z % 2), (0, z)]
    widths = [(2, (x + 2) % 4), (1, (x + 1) % 4), (1, (x + 3) % 4), (0, x)]
    pairs = sorted(
        ((far + wide, far, n, depth, width)
         for far, depth in depths
         for n, (wide, width) in enumerate(widths)),
        key=lambda pair: (-pair[0], -pair[1], pair[2]),
    )
    found = []
    for total, _, _, depth, width in pairs:
        for twin in (1 - core, core):
            if total > 0 or twin is not core:
                found.append((depth * 4 + width) * 2 + twin)
    return found


def kernel(
    atm, w1, bias, w2, edge, spread1, spread2, placed, fourier, phase, table, result,
    shifted, halo, w1_v, bias_v, w2_v, edge_v, spread1_v, spread2_v, fourier_v, phase_v, table_v,
    t1, t1h, t2, t2n, hsend, acc, hidden, mixed, packed, received,
    load_sem, halo_send, halo_recv, a2a_send, a2a_recv, rows_in,
):
    me = lax.axis_index("lat")
    barrier = pltpu.get_barrier_semaphore()

    loads = [
        (atm, shifted.at[pl.ds(256, 128), :]),
        (edge, edge_v),
        (w1, w1_v),
        (spread1, spread1_v),
        (bias, bias_v),
        (w2, w2_v),
        (spread2, spread2_v),
        (fourier, fourier_v),
        (placed, t2.at[:, pl.ds(640, 128)]),
        (phase, phase_v),
        (table.at[me], table_v),
    ]
    copies = [
        pltpu.make_async_copy(source, target, load_sem.at[n])
        for n, (source, target) in enumerate(loads)
    ]
    column, depth = me % 8, me // 8
    line = [8 * ((depth + k) % 4) + column for k in (1, 2, 3)]
    row = [8 * depth + (column + k) % 8 for k in (1, 7, 2, 6, 3, 5, 4)]

    def tell(semaphore, other):
        pl.semaphore_signal(
            semaphore, inc=1, device_id={"lat": other}, device_id_type=pl.DeviceIdType.MESH
        )

    step = jnp.where(column == 7, 1, -1)
    crossing = ((column == 7) & (me < BANDS - 1)) | ((column == 0) & (me > 0))

    for other in row[:2]:
        tell(barrier, other)

    @pl.when(crossing)
    def _():
        tell(barrier, me + step)

    copies[0].start()
    copies[1].start()
    for other in row[2:] + line:
        tell(barrier, other)

    for copy in copies[2:]:
        copy.start()

    copies[0].wait()
    copies[1].wait()
    hsend[...] = jnp.dot(
        edge_v[...], shifted[256:384, :], preferred_element_type=F32
    ).astype(BF16)

    pl.semaphore_wait(barrier, jnp.where(crossing, 11, 10))

    up = lax.max(me - 1, 0)
    down = lax.min(me + 1, BANDS - 1)
    to_up = pltpu.make_async_remote_copy(
        src_ref=hsend.at[pl.ds(0, 32), :], dst_ref=halo.at[1, pl.ds(64, 32), :],
        send_sem=halo_send.at[0], recv_sem=halo_recv.at[0],
        device_id={"lat": up}, device_id_type=pl.DeviceIdType.MESH,
    )
    to_down = pltpu.make_async_remote_copy(
        src_ref=hsend.at[pl.ds(32, 32), :], dst_ref=halo.at[0, pl.ds(64, 32), :],
        send_sem=halo_send.at[1], recv_sem=halo_recv.at[1],
        device_id={"lat": down}, device_id_type=pl.DeviceIdType.MESH,
    )

    @pl.when(me > 0)
    def _():
        to_up.start()

    @pl.when(me < BANDS - 1)
    def _():
        to_down.start()

    for other in line:
        tell(rows_in, other)

    copies[2].wait()
    copies[3].wait()
    res1 = jnp.dot(base_of(w1_v), spread1_v[...], preferred_element_type=F32).astype(BF16)
    for dx in range(5):
        for y in range(ROWS):
            t1[16 * y : 16 * y + 16, 128 * dx : 128 * dx + 128] = res1[
                16 * dx : 16 * dx + 16, 128 * y : 128 * y + 128
            ]
        for e in range(4):
            side, at = e // 2, 16 * (e % 2)
            start = 1024 + 64 * e + 32 * side
            t1h[side, at : at + 16, 32 * dx : 32 * dx + 32] = res1[
                16 * dx : 16 * dx + 16, start : start + 32
            ]

    own = shifted[256:384, :].astype(F32)
    for dx in (0, 1, 3, 4):
        shifted[128 * dx : 128 * dx + 128, :] = pltpu.roll(own, (2 - dx) % LON, 1).astype(BF16)
    copies[4].wait()
    eye = lax.broadcasted_iota(jnp.int32, (CH, CH), 0) == lax.broadcasted_iota(
        jnp.int32, (CH, CH), 1
    )
    column = jnp.sum(
        jnp.where(eye, jnp.broadcast_to(bias_v[...], (CH, CH)), 0.0), axis=1, keepdims=True
    )
    offsets = jnp.concatenate([column] * ROWS, axis=0)
    acc[...] = jnp.dot(t1[...], shifted[...], preferred_element_type=F32) + offsets
    hidden[32:96, :] = gelu(acc[32:96, :]).astype(BF16)

    copies[5].wait()
    copies[6].wait()
    res2 = jnp.dot(base_of(w2_v), spread2_v[...], preferred_element_type=F32).astype(BF16)
    for at, slot in enumerate(SLOTS):
        row = 16 * (slot % 16)
        for dx in range(5):
            t2[row : row + 16, 128 * dx : 128 * dx + 128] = res2[
                16 * dx : 16 * dx + 16, 128 * at : 128 * at + 128
            ]
    t2[160:224, 0:640] = jnp.zeros((64, 640), BF16)
    copies[7].wait()
    mixed[:, 640:768] = jnp.dot(
        shifted[256:384, :], fourier_v[...], preferred_element_type=F32
    ).T.astype(BF16)

    copies[8].wait()
    t2n[...] = t2[...].astype(F32).T.astype(BF16)

    @pl.when(me == 0)
    def _():
        halo[0, 64:96, :] = jnp.zeros((32, LON), BF16)

    @pl.when(me == BANDS - 1)
    def _():
        halo[1, 64:96, :] = jnp.zeros((32, LON), BF16)

    def edge_of(side):
        rim = halo[side, 64:96, :].astype(F32)
        for dx in (0, 1, 3, 4):
            halo[side, 32 * dx : 32 * dx + 32, :] = pltpu.roll(rim, (2 - dx) % LON, 1).astype(BF16)
        more = jnp.dot(t1h[side], halo[side], preferred_element_type=F32)
        rows = pl.ds(pl.multiple_of(96 * side, 32), 32)
        hidden[rows, :] = gelu(acc[rows, :] + more).astype(BF16)

    core = me % 2
    pl.when(core == 0)(to_up.wait_recv)
    pl.when(core == 1)(to_down.wait_recv)
    edge_of(1 - core)
    pl.when((core == 0) & (me > 0))(to_down.wait_recv)
    pl.when((core == 1) & (me < BANDS - 1))(to_up.wait_recv)
    edge_of(core)

    spectra = jnp.dot(hidden[...], fourier_v[...], preferred_element_type=F32).T
    whole, crossing_parts = spectra, pltpu.roll(spectra.reshape(BANDS, 8, 128), 4, 1)
    crossing_parts = crossing_parts.reshape(256, 128)
    copies[9].wait()
    others = peers(me)

    def send(p):
        pltpu.make_async_remote_copy(
            src_ref=packed.at[p], dst_ref=received.at[me],
            send_sem=a2a_send, recv_sem=a2a_recv,
            device_id={"lat": p}, device_id_type=pl.DeviceIdType.MESH,
        ).start()

    for low, high in ((0, 8), (8, BANDS)):
        rows = slice(8 * low, 8 * high)
        spectra, swapped = whole[rows], crossing_parts[rows]
        mixed[rows, 256:384] = spectra.astype(BF16)
        for shift, less, more in ((1, 1, 3), (2, 0, 4)):
            straight = phase_v[2 * shift - 2, rows, :] * spectra
            crossed = phase_v[2 * shift - 1, rows, :] * swapped
            mixed[rows, 128 * more : 128 * more + 128] = (straight + crossed).astype(BF16)
            mixed[rows, 128 * less : 128 * less + 128] = (straight - crossed).astype(BF16)
        sums = jnp.dot(mixed[rows, :], t2n[...], preferred_element_type=F32)
        sums = sums.reshape(high - low, 8, 256)
        near = swap_blocks(sums[:, :, 0:128])
        far = swap_blocks(sums[:, :, 128:256])
        packed[low:high] = jnp.concatenate([near, far], axis=1).astype(BF16)
        if low == 0:
            pl.semaphore_wait(rows_in, 3)
            pl.when(me != 1)(functools.partial(send, 1))
        for p in others:
            pl.when((p != 1) & (p >= low) & (p < high))(functools.partial(send, p))

    received[me] = packed[me]
    copies[10].wait()
    some = pltpu.make_async_remote_copy(
        src_ref=packed.at[pl.ds(0, BANDS - 1)], dst_ref=received.at[pl.ds(0, BANDS - 1)],
        send_sem=a2a_send, recv_sem=a2a_recv,
        device_id={"lat": lax.rem(me + 1, BANDS)}, device_id_type=pl.DeviceIdType.MESH,
    )
    some.wait_recv()

    parts = received[...].astype(F32)
    near = parts[:, 0:8, :]
    far = parts[:, 8:16, :]
    none = jnp.zeros((1, 8, 128), F32)
    above = jnp.concatenate([none, far[:-1]], axis=0)
    below = jnp.concatenate([far[1:], none], axis=0)
    first = lax.broadcasted_iota(jnp.int32, near.shape, 1) < 4
    rows = (near + jnp.where(first, above, below)).reshape(LAT, 128)
    lines = rows.T.astype(BF16)
    for m in range(OWN):
        left = jnp.concatenate([lines[16 * m : 16 * m + 16], lines[64 + 16 * m : 80 + 16 * m]], axis=0)
        done = jnp.dot(left, table_v[m], preferred_element_type=F32)
        for q in range(2):
            for a in range(2):
                result[m, q, pl.ds(a, CH, stride=2), :] = done[
                    16 * a : 16 * a + 16, 128 * q : 128 * q + 128
                ]
    some.wait_send()
    pl.when(me > 0)(to_up.wait_send)
    pl.when(me < BANDS - 1)(to_down.wait_send)


def store(source, target, semaphore):
    copy = pltpu.make_async_copy(source, target, semaphore)
    copy.start()
    copy.wait()


@functools.cache
def constants():
    return (
        edge_rows(), spread_first(), spread_second(), placed_rows(), fourier_rows(),
        phase_rows(), projection_table(),
    )


def per_device(atmosphere, first_weight, first_bias, second_weight):
    edge, spread1, spread2, placed, fourier, phase, table = constants()
    operands = (
        atmosphere.reshape(CH * ROWS, LON),
        first_weight.transpose(2, 3, 0, 1),
        first_bias.reshape(1, CH),
        second_weight.transpose(2, 3, 0, 1),
        edge, spread1, spread2, placed, fourier, phase, table,
    )
    scratch = [
        pltpu.VMEM((640, LON), BF16),
        pltpu.VMEM((2, 160, LON), BF16),
        pltpu.VMEM((5, 5, CH, CH), BF16),
        pltpu.VMEM((1, CH), F32),
        pltpu.VMEM((5, 5, CH, CH), BF16),
        pltpu.VMEM(edge.shape, BF16),
        pltpu.VMEM(spread1.shape, BF16),
        pltpu.VMEM(spread2.shape, BF16),
        pltpu.VMEM(fourier.shape, BF16),
        pltpu.VMEM(phase.shape, F32),
        pltpu.VMEM(table.shape[1:], BF16),
        pltpu.VMEM((128, 640), BF16),
        pltpu.VMEM((2, 32, 160), BF16),
        pltpu.VMEM((256, 768), BF16),
        pltpu.VMEM((768, 256), BF16),
        pltpu.VMEM((64, LON), BF16),
        pltpu.VMEM((128, LON), F32),
        pltpu.VMEM((128, LON), BF16),
        pltpu.VMEM((256, 768), BF16),
        pltpu.VMEM((BANDS, 16, 128), BF16),
        pltpu.VMEM((BANDS, 16, 128), BF16),
        pltpu.SemaphoreType.DMA((11,)),
        pltpu.SemaphoreType.DMA((2,)),
        pltpu.SemaphoreType.DMA((2,)),
        pltpu.SemaphoreType.DMA,
        pltpu.SemaphoreType.DMA,
        pltpu.SemaphoreType.REGULAR,
    ]
    spectrum = pl.pallas_call(
        kernel,
        out_shape=pltpu.VMEM((OWN, 2, 2 * CH, 128), F32),
        in_specs=[pl.BlockSpec(memory_space=pltpu.HBM)] * len(operands),
        out_specs=pl.BlockSpec(memory_space=pltpu.VMEM),
        scratch_shapes=scratch,
        compiler_params=pltpu.CompilerParams(
            collective_id=0, has_side_effects=True, vmem_limit_bytes=56 * 1024 * 1024
        ),
        name="encoder",
    )(*operands)
    spectrum = pl.pallas_call(
        store,
        out_shape=jax.ShapeDtypeStruct((OWN, 2, 2 * CH, 128), F32),
        in_specs=[pl.BlockSpec(memory_space=pl.ANY)],
        compiler_params=pltpu.CompilerParams(vmem_limit_bytes=1024 * 1024),
        out_specs=pl.BlockSpec(memory_space=pltpu.HBM),
        scratch_shapes=[pltpu.SemaphoreType.DMA],
        name="store",
    )(spectrum)
    return spectrum.reshape(OWN, 2, CH, 2, 128)


def solution(mesh):
    placed = (
        P("chan", "lat", None),
        P("chan", None, None, None),
        P("chan"),
        P("chan", None, None, None),
    )
    return jax.shard_map(
        per_device,
        mesh=mesh,
        in_specs=placed,
        out_specs=P("lat", None, "chan", None, None),
        check_vma=False,
    )
```
